128 devices in a mesh: sample: 8 (over y, x_hi), tok: 16 (over z, x_lo, core).
Axes of the slice: x: 4 (x_hi: 2, x_lo: 2; x = x_hi * 2 + x_lo), y: 4, z: 4, core: 2. Of those that a mesh axis runs over, the one named last changes fastest.
Arguments:
- single: bfloat16 [32, 1024, 768], P('sample', 'tok'), may hold values from -6 to 6
- pair: bfloat16 [1024, 1024, 128], P('tok', 'sample'), may hold values from -400 to 400
- w_query: bfloat16 [768, 768], replicated, may hold values from -0.21875 to 0.21875
- w_key: bfloat16 [768, 768], replicated, may hold values from -0.21875 to 0.21875
- w_value: bfloat16 [768, 768], replicated, may hold values from -0.21875 to 0.21875
- w_out: bfloat16 [768, 768], replicated, may hold values from -0.21875 to 0.21875
- w_pair: bfloat16 [128, 16], replicated, may hold values from -0.5 to 0.5
- cotangent: bfloat16 [32, 1024, 768], P('sample', 'tok'), may hold values from -64 to 64
Outputs:
- grad_single: bfloat16 [32, 1024, 768], P('sample', 'tok')
- grad_pair: bfloat16 [1024, 1024, 128], P('tok', 'sample')
The draws below stay inside these ranges and needn't reach their ends.
All inputs are finite; a program needn't handle non-finite values.
Results may differ from the reference program's by a relative error of at most 0.02.
Values may be sent and summed in bfloat16 or wider, within the bound.
No kernel may reach another device: no remote copies, remote signals or barrier semaphores. Data moves between devices by JAX's collectives and lax.ppermute only.
A program may use at most 128 MiB of HBM per device.

```python
import math
import jax
import jax.numpy as jnp
from jax import lax

WIDTH = 768
HEADS = 16
HEAD_DIM = 48
PAIR_DIM = 128
TOK_DEV = 64
TOKENS = 1024
SAMPLES = 32
N_TOK = 16


def draw_pair(key, part):
    key = jax.random.fold_in(key, 11)
    base_key = jax.random.fold_in(key, 0)
    shape_full = (TOKENS, TOKENS, PAIR_DIM)
    value = jax.random.truncated_normal(base_key, -4.0, 4.0, shape_full, jnp.float32)
    return value.astype(jnp.bfloat16)


def levels(key, shape, cuts, smallest, top_value):
    level, own = 1.0, jax.random.fold_in(key, 6)
    for position, parts in cuts:
        heights = jnp.exp(jax.random.uniform(jax.random.fold_in(own, position), (parts,), jnp.float32, smallest / len(cuts), top_value / len(cuts)))
        level = level * jnp.repeat(heights, shape[position] // parts).reshape([-1 if axis == position else 1 for axis in range(len(shape))])
    return level


def centred(stream_key, shape, scale, reach, cuts=(), held_as=jnp.bfloat16):
    loudness = levels(stream_key, shape, cuts, -0.22, 0.18) if cuts else 1.0
    result = jax.random.normal(stream_key, shape, jnp.float32) * scale * loudness
    return jnp.minimum(jnp.maximum(result, -reach), reach).astype(held_as)


def setup_inputs(seed: int = 0) -> dict:
    seeds = jax.random.split(jax.random.key(seed), 9)
    return {
        "single": centred(seeds[0], (SAMPLES, TOKENS, WIDTH), 1.0, 6.0, ((0, 8), (1, 16))),
        "pair": draw_pair(jax.random.fold_in(seeds[8], 71), 0),
        "w_query": centred(seeds[2], (WIDTH, WIDTH), WIDTH ** -0.5, 0.21875),
        "w_key": centred(seeds[3], (WIDTH, WIDTH), WIDTH ** -0.5, 0.21875),
        "w_value": centred(seeds[4], (WIDTH, WIDTH), WIDTH ** -0.5, 0.21875),
        "w_out": centred(seeds[5], (WIDTH, WIDTH), WIDTH ** -0.5, 0.21875),
        "w_pair": centred(seeds[6], (PAIR_DIM, HEADS), PAIR_DIM ** -0.5, 0.5),
        "cotangent": centred(seeds[7], (SAMPLES, TOKENS, WIDTH), 16.0, 64.0, ((0, 8), (1, 16))),
    }


def reference(single, pair, w_query, w_key, w_value, w_out, w_pair, cotangent):
    score_scale = 1.0 / math.sqrt(HEAD_DIM)
    pair_bias = jnp.dot(pair.reshape(TOKENS * TOKENS, PAIR_DIM), w_pair, preferred_element_type=jnp.float32)
    pair_bias = pair_bias.reshape(TOKENS, TOKENS, HEADS).transpose(2, 0, 1)

    def one_sample(running, inputs):
        single_rows, cot_rows = inputs
        queries = jnp.dot(single_rows, w_query, preferred_element_type=jnp.float32).astype(jnp.bfloat16)
        keys = jnp.dot(single_rows, w_key, preferred_element_type=jnp.float32).astype(jnp.bfloat16)
        values = jnp.dot(single_rows, w_value, preferred_element_type=jnp.float32).astype(jnp.bfloat16)
        out_grads = jnp.dot(cot_rows, w_out.T, preferred_element_type=jnp.float32).astype(jnp.bfloat16)
        query_heads = queries.astype(jnp.float32).reshape(TOKENS, HEADS, HEAD_DIM)
        key_heads = keys.astype(jnp.float32).reshape(TOKENS, HEADS, HEAD_DIM)
        value_heads = values.astype(jnp.float32).reshape(TOKENS, HEADS, HEAD_DIM)
        out_heads = out_grads.astype(jnp.float32).reshape(TOKENS, HEADS, HEAD_DIM)
        scores = jnp.einsum('ihd,jhd->hij', query_heads, key_heads) * score_scale + pair_bias
        probs = jax.nn.softmax(scores, axis=-1)
        probs_low = probs.astype(jnp.bfloat16)
        grad_probs = jnp.einsum('ihd,jhd->hij', out_heads, value_heads)
        row_dot = lax.optimization_barrier(jnp.sum(probs * grad_probs, axis=-1, keepdims=True))
        grad_scores = probs * (grad_probs - row_dot)
        grad_low = grad_scores.astype(jnp.bfloat16)
        grad_query = (jnp.einsum('hij,jhd->ihd', grad_low.astype(jnp.float32), key_heads) * score_scale).astype(jnp.bfloat16)
        grad_query = grad_query.reshape(TOKENS, WIDTH)
        score_blocks = grad_low.astype(jnp.float32).reshape(HEADS, N_TOK, TOK_DEV, TOKENS)
        query_blocks = query_heads.reshape(N_TOK, TOK_DEV, HEADS, HEAD_DIM)
        key_block = (jnp.einsum('hnij,nihd->njhd', score_blocks, query_blocks) * score_scale).astype(jnp.bfloat16)
        prob_blocks = probs_low.astype(jnp.float32).reshape(HEADS, N_TOK, TOK_DEV, TOKENS)
        out_blocks = out_heads.reshape(N_TOK, TOK_DEV, HEADS, HEAD_DIM)
        value_block = jnp.einsum('hnij,nihd->njhd', prob_blocks, out_blocks).astype(jnp.bfloat16)
        mapped = jnp.dot(key_block.reshape(N_TOK * TOKENS, WIDTH), w_key.T, preferred_element_type=jnp.float32)
        mapped = mapped + jnp.dot(value_block.reshape(N_TOK * TOKENS, WIDTH), w_value.T, preferred_element_type=jnp.float32)
        mapped = lax.optimization_barrier(mapped.astype(jnp.bfloat16)).astype(jnp.float32)
        key_value_grad = lax.optimization_barrier(jnp.sum(mapped.reshape(N_TOK, TOKENS, WIDTH), axis=0))
        grad_rows = jnp.dot(grad_query, w_query.T, preferred_element_type=jnp.float32) + key_value_grad
        return (running + grad_scores, grad_rows.astype(jnp.bfloat16))
    start_grad = jnp.zeros((HEADS, TOKENS, TOKENS), jnp.float32)
    bias_grad, grad_single = lax.scan(one_sample, start_grad, (single, cotangent))
    bias_low = bias_grad.astype(jnp.bfloat16)
    grad_pair = jnp.dot(bias_low.transpose(1, 2, 0).reshape(TOKENS * TOKENS, HEADS), w_pair.T, preferred_element_type=jnp.float32)
    grad_pair = grad_pair.astype(jnp.bfloat16).reshape(TOKENS, TOKENS, PAIR_DIM)
    return (grad_single, grad_pair)
```

```python
import math
import functools
import jax, jax.numpy as jnp
from jax import lax
from jax.experimental import pallas as pl
from jax.experimental.pallas import tpu as pltpu
from jax.sharding import PartitionSpec as P

F32 = jnp.float32
BF16 = jnp.bfloat16
LOG2E = 1.4426950408889634
NB = 4
HEADS = 16
WIDTH = 768
HD = 48
TOK = 1024


def prep_body(order_ref, r_ref, q_ref, o_ref, qt_ref, ot_ref, kt_ref, vt_ref, k_ref):
    def piece(slot, first, sample):
        lanes = slice(sample * 64, sample * 64 + 64)
        return jnp.concatenate([r_ref[first, slot, :, lanes], r_ref[first + 1, slot, :, lanes]], axis=1)

    def turned(block):
        return block.astype(F32).T.astype(BF16)

    for u in range(8):
        cols = slice(u * 128, u * 128 + 128)
        other = order_ref[u] * 2
        for b in range(NB):
            qt = piece(0, 2 * u, b)
            qt_ref[b, :, cols] = qt
            q_ref[b, cols, :] = turned(qt)
            ot = piece(3, 2 * u, b)
            ot_ref[b, :, cols] = ot
            o_ref[b, cols, :] = turned(ot)
            kt = piece(1, other, b)
            kt_ref[b, :, cols] = kt
            k_ref[b, cols, :] = turned(kt)
            vt_ref[b, :, cols] = piece(2, other, b)


def prep(order, received):
    nat = jax.ShapeDtypeStruct((NB, TOK, HD), BF16)
    tr = jax.ShapeDtypeStruct((NB, HD, TOK), BF16)
    vm = pl.BlockSpec(memory_space=pltpu.VMEM)
    return pl.pallas_call(
        prep_body,
        out_shape=[nat, nat, tr, tr, tr, tr, nat],
        in_specs=[pl.BlockSpec(memory_space=pltpu.SMEM), vm],
        out_specs=[vm] * 7,
        compiler_params=pltpu.CompilerParams(vmem_limit_bytes=32 * 2**20),
        name="prep",
    )(order, received)


TILE = 256


def attend_body(scale, steps, order_ref, bias_ref, q_ref, o_ref, qt_ref, ot_ref, kt_ref, vt_ref, k_ref,
                dbias_ref, g_ref, s_ref, dp_ref, p_ref, ds_ref, acc_ref, dqt_ref, dkt_ref, dvt_ref):
    step = pl.program_id(0)

    @pl.when(step == 0)
    def _():
        dkt_ref[...] = jnp.zeros_like(dkt_ref)
        dvt_ref[...] = jnp.zeros_like(dvt_ref)

    G = 16
    for b in range(NB):
        s_ref[b % 2] = jnp.dot(q_ref[b], kt_ref[b], preferred_element_type=F32)
        dp_ref[b % 2] = jnp.dot(o_ref[b], vt_ref[b], preferred_element_type=F32)
        for g in range(TILE // G):
            rows = slice(g * G, g * G + G)
            bias = jnp.concatenate([bias_ref[u, rows, :] for u in range(8)], axis=1)
            s = s_ref[b % 2, rows, :] * (scale * LOG2E) + bias
            m = jnp.max(s, axis=1, keepdims=True)
            e = jnp.exp2(s - m)
            inv = 1.0 / jnp.sum(e, axis=1, keepdims=True)
            p = e * inv
            dp = dp_ref[b % 2, rows, :]
            rd = jnp.sum(p * dp, axis=1, keepdims=True)
            ds = p * (dp - rd)
            p_ref[b % 2, rows, :] = p.astype(BF16)
            ds_ref[b % 2, rows, :] = ds.astype(BF16)
            if b == 0:
                acc_ref[rows, :] = ds
            elif b < NB - 1:
                acc_ref[rows, :] += ds
            else:
                tot = (acc_ref[rows, :] + ds).astype(BF16)
                for u in range(8):
                    dbias_ref[u, rows, :] = tot[:, u * 128:u * 128 + 128]
        pl_, dl = p_ref[b % 2], ds_ref[b % 2]
        dkt_ref[b] += jnp.dot(qt_ref[b], dl, preferred_element_type=F32)
        dvt_ref[b] += jnp.dot(ot_ref[b], pl_, preferred_element_type=F32)
        dq = jnp.dot(dl, k_ref[b], preferred_element_type=F32)
        dqt_ref[step, b] = (dq * scale).T.astype(BF16)

    @pl.when(step == steps - 1)
    def _():
        for b in range(NB):
            lanes = slice(b * 64, b * 64 + 64)
            for t in range(16):
                c = (t % 4) * 64
                g_ref[t, 0, :, lanes] = dqt_ref[t // 4, b, :, c:c + 64]
            for u in range(8):
                first = order_ref[u] * 2
                dk = (dkt_ref[b, :, u * 128:u * 128 + 128] * scale).astype(BF16)
                dv = dvt_ref[b, :, u * 128:u * 128 + 128].astype(BF16)
                g_ref[first, 1, :, lanes] = dk[:, :64]
                g_ref[first + 1, 1, :, lanes] = dk[:, 64:]
                g_ref[first, 2, :, lanes] = dv[:, :64]
                g_ref[first + 1, 2, :, lanes] = dv[:, 64:]


def attend(order, bias, q, o, qt, ot, kt, vt, k):
    steps = TOK // TILE
    scale = 1.0 / math.sqrt(HD)
    nat_t = pl.BlockSpec((NB, TILE, HD), lambda i: (0, i, 0))
    tr_t = pl.BlockSpec((NB, HD, TILE), lambda i: (0, 0, i))
    tr_w = pl.BlockSpec((NB, HD, TOK), lambda i: (0, 0, 0))
    nat_w = pl.BlockSpec((NB, TOK, HD), lambda i: (0, 0, 0))
    bias_t = pl.BlockSpec((8, TILE, 128), lambda i: (0, i, 0))
    return pl.pallas_call(
        functools.partial(attend_body, scale, steps),
        grid=(steps,),
        out_shape=[jax.ShapeDtypeStruct((8, TOK, 128), BF16), jax.ShapeDtypeStruct((16, 3, HD, 256), BF16)],
        in_specs=[pl.BlockSpec(memory_space=pltpu.SMEM), bias_t, nat_t, nat_t, tr_t, tr_t, tr_w, tr_w, nat_w],
        out_specs=[bias_t, pl.BlockSpec((16, 3, HD, 256), lambda i: (0, 0, 0, 0))],
        scratch_shapes=[
            pltpu.VMEM((2, TILE, TOK), F32), pltpu.VMEM((2, TILE, TOK), F32),
            pltpu.VMEM((2, TILE, TOK), BF16), pltpu.VMEM((2, TILE, TOK), BF16),
            pltpu.VMEM((TILE, TOK), F32), pltpu.VMEM((steps, NB, HD, TILE), BF16),
            pltpu.VMEM((NB, HD, TOK), F32), pltpu.VMEM((NB, HD, TOK), F32),
        ],
        compiler_params=pltpu.CompilerParams(vmem_limit_bytes=48 * 2**20),
        name="attend",
    )(order, bias, q, o, qt, ot, kt, vt, k)


def bias_body(pair_ref, w_ref, out_ref):
    for g in range(8):
        cols = jnp.concatenate([pair_ref[g * 8 + r] for r in range(8)], axis=1)
        t = lax.dot_general(w_ref[...], cols, (((1,), (1,)), ((), ())), preferred_element_type=F32)
        t = t * LOG2E
        for h in range(16):
            out_ref[h, g * 8:g * 8 + 8, :] = t[h * 8:h * 8 + 8, :]


def bias_part(pair, w_pair):
    eye = jnp.eye(8, dtype=BF16)
    w = (w_pair.T[:, None, None, :] * eye[None, :, :, None]).reshape(128, 1024)
    vm = pl.BlockSpec(memory_space=pltpu.VMEM)
    return pl.pallas_call(
        bias_body, out_shape=jax.ShapeDtypeStruct((16, 64, 128), F32),
        in_specs=[vm, vm], out_specs=vm,
        compiler_params=pltpu.CompilerParams(vmem_limit_bytes=32 * 2**20), name="bias_part",
    )(pair, w)


def gpair_body(x_ref, w_ref, out_ref):
    for g in range(4):
        x = x_ref[:, g * 16:g * 16 + 16, :].reshape(256, 128)
        t = lax.dot_general(x, w_ref[...], (((0,), (0,)), ((), ())), preferred_element_type=F32)
        for r in range(16):
            out_ref[g * 16 + r] = t[:, r * 128:r * 128 + 128].astype(BF16)


def gpair(x, w_pair):
    eye = jnp.eye(16, dtype=BF16)
    w = (w_pair.T[:, None, None, :] * eye[None, :, :, None]).reshape(256, 2048)
    vm = pl.BlockSpec(memory_space=pltpu.VMEM)
    return pl.pallas_call(
        gpair_body, out_shape=jax.ShapeDtypeStruct((64, 128, 128), BF16),
        in_specs=[vm, vm], out_specs=vm,
        compiler_params=pltpu.CompilerParams(vmem_limit_bytes=32 * 2**20), name="gpair",
    )(x, w)


def project_body(x_ref, c_ref, wq_ref, wk_ref, wv_ref, wo_ref, out_ref):
    x = x_ref[...].reshape(NB * 64, WIDTH)
    c = c_ref[...].reshape(NB * 64, WIDTH)
    for slot, w_ref in enumerate((wq_ref, wk_ref, wv_ref)):
        t = jnp.dot(x, w_ref[...], preferred_element_type=F32).T.astype(BF16)
        for h in range(HEADS):
            out_ref[h, slot] = t[h * HD:h * HD + HD, :]
    t = lax.dot_general(wo_ref[...], c, (((1,), (1,)), ((), ())), preferred_element_type=F32).astype(BF16)
    for h in range(HEADS):
        out_ref[h, 3] = t[h * HD:h * HD + HD, :]


def project(single, cotangent, w_query, w_key, w_value, w_out):
    vm = pl.BlockSpec(memory_space=pltpu.VMEM)
    return pl.pallas_call(
        project_body, out_shape=jax.ShapeDtypeStruct((HEADS, 4, HD, NB * 64), BF16),
        in_specs=[vm] * 6, out_specs=vm,
        compiler_params=pltpu.CompilerParams(vmem_limit_bytes=40 * 2**20), name="project",
    )(single, cotangent, w_query, w_key, w_value, w_out)


def final_body(g_ref, wq_ref, wk_ref, wv_ref, out_ref):
    total = None
    for slot, w_ref in enumerate((wq_ref, wk_ref, wv_ref)):
        part = jnp.dot(w_ref[...], g_ref[:, slot].reshape(WIDTH, NB * 64), preferred_element_type=F32)
        total = part if total is None else total + part
    out_ref[...] = total.T.astype(BF16).reshape(NB, 64, WIDTH)


def final(g, w_query, w_key, w_value):
    vm = pl.BlockSpec(memory_space=pltpu.VMEM)
    return pl.pallas_call(
        final_body, out_shape=jax.ShapeDtypeStruct((NB, 64, WIDTH), BF16),
        in_specs=[vm] * 4, out_specs=vm,
        compiler_params=pltpu.CompilerParams(vmem_limit_bytes=40 * 2**20), name="final",
    )(g, w_query, w_key, w_value)


def shift_y(x, d):
    return lax.ppermute(x, "sample", [(i, ((i // 2 + d) % 4) * 2 + i % 2) for i in range(8)])


def swap_x(x):
    return lax.ppermute(x, "sample", [(i, i ^ 1) for i in range(8)])


def gather_blocks(own):
    half = own.shape[0] // 2
    pair = [own, swap_x(own)]
    up = [shift_y(v, 1) for v in pair]
    down = [shift_y(v, -1) for v in pair]
    far = [jnp.concatenate([shift_y(u[:half], 1), shift_y(d[half:], -1)]) for u, d in zip(up, down)]
    return jnp.stack(pair + up + down + far)


def key_order():
    me = lax.axis_index("sample")
    y, x = me // 2, me % 2
    return jnp.stack([((y + d) % 4) * 2 + (x ^ e) for d in (0, 3, 1, 2) for e in (0, 1)]).astype(jnp.int32)


def plus(a, b):
    return (a.astype(F32) + b.astype(F32)).astype(BF16)


def scatter_blocks(blocks):
    half = blocks.shape[1] // 2
    sums = []
    for e in (1, 0):
        far, up, down = blocks[6 + e], blocks[4 + e], blocks[2 + e]
        from_down = shift_y(far[:half], 1)
        from_up = shift_y(far[half:], -1)
        up = jnp.concatenate([plus(up[:half], from_down), up[half:]])
        down = jnp.concatenate([down[:half], plus(down[half:], from_up)])
        total = blocks[e].astype(F32) + shift_y(up, 1).astype(F32) + shift_y(down, -1).astype(F32)
        sums.append(total)
    return (sums[1] + swap_x(sums[0].astype(BF16)).astype(F32)).astype(BF16)


def local(single, pair, w_query, w_key, w_value, w_out, w_pair, cotangent):
    order = key_order()
    bias = lax.all_to_all(bias_part(pair, w_pair), "tok", 0, 0).reshape(TOK, 128)
    bias = gather_blocks(bias)
    sent = project(single, cotangent, w_query, w_key, w_value, w_out)
    held = prep(order, lax.all_to_all(sent, "tok", 0, 0))
    dbias, grads = attend(order, bias, *held)
    grads = lax.all_to_all(grads, "tok", 0, 0)
    grad_single = final(grads, w_query, w_key, w_value)
    dbias = scatter_blocks(dbias).reshape(16, 64, 128)
    grad_pair = gpair(lax.all_to_all(dbias, "tok", 0, 0), w_pair)
    return (grad_single, grad_pair)


def solution(mesh):
    rows, keys = P("sample", "tok", None), P("tok", "sample", None)
    return jax.shard_map(
        local, mesh=mesh, in_specs=(rows, keys, P(), P(), P(), P(), P(), rows),
        out_specs=(rows, keys), check_vma=False,
    )
```

```python
import math
import functools
import jax, jax.numpy as jnp
from jax import lax
from jax.experimental import pallas as pl
from jax.experimental.pallas import tpu as pltpu
from jax.sharding import PartitionSpec as P

F32 = jnp.float32
BF16 = jnp.bfloat16
LOG2E = 1.4426950408889634
NB = 4
HEADS = 16
WIDTH = 768
HD = 48
TOK = 1024


def prep_body(order_ref, r_ref, q_ref, o_ref, qt_ref, ot_ref, kt_ref, vt_ref, k_ref):
    def piece(slot, first, sample):
        lanes = slice(sample * 64, sample * 64 + 64)
        return jnp.concatenate([r_ref[first, slot, :, lanes], r_ref[first + 1, slot, :, lanes]], axis=1)

    def turned(block):
        return block.astype(F32).T.astype(BF16)

    for u in range(8):
        cols = slice(u * 128, u * 128 + 128)
        other = order_ref[u] * 2
        for b in range(NB):
            qt = piece(0, 2 * u, b)
            qt_ref[b, :, cols] = qt
            q_ref[b, cols, :] = turned(qt)
            ot = piece(3, 2 * u, b)
            ot_ref[b, :, cols] = ot
            o_ref[b, cols, :] = turned(ot)
            kt = piece(1, other, b)
            kt_ref[b, :, cols] = kt
            k_ref[b, cols, :] = turned(kt)
            vt_ref[b, :, cols] = piece(2, other, b)


def prep(order, received):
    nat = jax.ShapeDtypeStruct((NB, TOK, HD), BF16)
    tr = jax.ShapeDtypeStruct((NB, HD, TOK), BF16)
    vm = pl.BlockSpec(memory_space=pltpu.VMEM)
    return pl.pallas_call(
        prep_body,
        out_shape=[nat, nat, tr, tr, tr, tr, nat],
        in_specs=[pl.BlockSpec(memory_space=pltpu.SMEM), vm],
        out_specs=[vm] * 7,
        compiler_params=pltpu.CompilerParams(vmem_limit_bytes=32 * 2**20),
        name="prep",
    )(order, received)


TILE = 256
VMEM_ATT = 40
CHUNKS = 2


def attend_body(scale, steps, chunk, order_ref, *refs):
    first, last = chunk == 0, chunk == CHUNKS - 1
    bias_refs, refs = refs[:5], refs[5:]
    (q_ref, o_ref, qt_ref, ot_ref, kt_ref, vt_ref, k_ref), refs = refs[:7], refs[7:]
    if not first:
        (g_in, dk_in, dv_in), refs = refs[:3], refs[11:]
    dbias_refs, refs = refs[:8], refs[8:]
    g_ref, dkt_ref, dvt_ref, s_ref, dp_ref, p_ref, ds_ref, acc_ref, dqt_ref = refs
    step = pl.program_id(0)

    @pl.when(step == 0)
    def _():
        dkt_ref[...] = jnp.zeros_like(dkt_ref) if first else dk_in[...]
        dvt_ref[...] = jnp.zeros_like(dvt_ref) if first else dv_in[...]

    def products(b):
        s_ref[b % 2] = jnp.dot(q_ref[b], kt_ref[b], preferred_element_type=F32)
        dp_ref[b % 2] = jnp.dot(o_ref[b], vt_ref[b], preferred_element_type=F32)

    def softmax(b):
        group = 16
        for g in range(TILE // group):
            rows = slice(g * group, g * group + group)
            bias = [ref[e, rows, :] for ref in bias_refs[:3] for e in range(2)] + [ref[rows, :] for ref in bias_refs[3:]]
            bias = jnp.concatenate(bias, axis=1)
            s = s_ref[b % 2, rows, :] * (scale * LOG2E) + bias
            m = jnp.max(s, axis=1, keepdims=True)
            e = jnp.exp2(s - m)
            inv = 1.0 / jnp.sum(e, axis=1, keepdims=True)
            p = e * inv
            dp = dp_ref[b % 2, rows, :]
            rd = jnp.sum(p * dp, axis=1, keepdims=True)
            ds = p * (dp - rd)
            p_ref[b % 2, rows, :] = p.astype(BF16)
            ds_ref[b % 2, rows, :] = ds.astype(BF16)
            if b == 0:
                acc_ref[rows, :] = ds
            elif b < NB - 1:
                acc_ref[rows, :] += ds
            else:
                total = (acc_ref[rows, :] + ds).astype(BF16)
                for u in range(8):
                    dbias_refs[u][rows, :] = total[:, u * 128:u * 128 + 128]

    def gradients(b):
        p_low, ds_low = p_ref[b % 2], ds_ref[b % 2]
        dkt_ref[b] += jnp.dot(qt_ref[b], ds_low, preferred_element_type=F32)
        dvt_ref[b] += jnp.dot(ot_ref[b], p_low, preferred_element_type=F32)
        dq = jnp.dot(ds_low, k_ref[b], preferred_element_type=F32)
        dqt_ref[step, b] = (dq * scale).T.astype(BF16)

    products(0)
    for b in range(NB):
        if b + 1 < NB:
            products(b + 1)
        softmax(b)
        if b:
            gradients(b - 1)
    gradients(NB - 1)

    @pl.when(step == steps - 1)
    def _():
        each = TILE // 64
        if not first:
            for t in range(chunk * steps * each):
                g_ref[t, 0] = g_in[t]
        for b in range(NB):
            lanes = slice(b * 64, b * 64 + 64)
            for t in range(steps * each):
                c = (t % each) * 64
                block = dqt_ref[t // each, b, :, c:c + 64]
                if last:
                    g_ref[chunk * steps * each + t, 0, :, lanes] = block
                else:
                    g_ref[t, :, lanes] = block
            if last:
                for u in range(8):
                    one = order_ref[u] * 2
                    dk = (dkt_ref[b, :, u * 128:u * 128 + 128] * scale).astype(BF16)
                    dv = dvt_ref[b, :, u * 128:u * 128 + 128].astype(BF16)
                    g_ref[one, 1, :, lanes] = dk[:, :64]
                    g_ref[one + 1, 1, :, lanes] = dk[:, 64:]
                    g_ref[one, 2, :, lanes] = dv[:, :64]
                    g_ref[one + 1, 2, :, lanes] = dv[:, 64:]


def attend(chunk, order, bias, held, dbias, carried):
    rows = TOK // CHUNKS
    steps = rows // TILE
    at = chunk * steps
    last = chunk == CHUNKS - 1
    scale = 1.0 / math.sqrt(HD)
    nat_t = pl.BlockSpec((NB, TILE, HD), lambda i: (0, i + at, 0))
    tr_t = pl.BlockSpec((NB, HD, TILE), lambda i: (0, 0, i + at))
    tr_w = pl.BlockSpec((NB, HD, TOK), lambda i: (0, 0, 0))
    nat_w = pl.BlockSpec((NB, TOK, HD), lambda i: (0, 0, 0))
    bias_t = [pl.BlockSpec((2, TILE, 128), lambda i: (0, i, 0))] * 3 + [pl.BlockSpec((TILE, 128), lambda i: (i, 0))] * 2
    dbias_t = pl.BlockSpec((TILE, 128), lambda i: (i + at, 0))
    g_spec = pl.BlockSpec((16, 3, HD, 256), lambda i: (0, 0, 0, 0))
    dq_spec = pl.BlockSpec((16 // CHUNKS, HD, 256), lambda i: (0, 0, 0))
    sums = jax.ShapeDtypeStruct((NB, HD, TOK), F32)
    in_specs = [pl.BlockSpec(memory_space=pltpu.SMEM)] + bias_t + [nat_t, nat_t, tr_t, tr_t, tr_w, tr_w, nat_w]
    aliases = {}
    if chunk:
        in_specs += [dq_spec, tr_w, tr_w]
        aliases = {len(in_specs) + u: u for u in range(8)}
        in_specs += [pl.BlockSpec(memory_space=pl.ANY)] * 8
    out_shape, out_specs = [pltpu.HBM((TOK, 128), BF16)] * 8, [dbias_t] * 8
    scratch = [
        pltpu.VMEM((2, TILE, TOK), F32), pltpu.VMEM((2, TILE, TOK), F32),
        pltpu.VMEM((2, TILE, TOK), BF16), pltpu.VMEM((2, TILE, TOK), BF16),
        pltpu.VMEM((TILE, TOK), F32), pltpu.VMEM((steps, NB, HD, TILE), BF16),
    ]
    if last:
        out_shape, out_specs = out_shape + [jax.ShapeDtypeStruct((16, 3, HD, 256), BF16)], out_specs + [g_spec]
        scratch = [pltpu.VMEM((NB, HD, TOK), F32)] * 2 + scratch
    else:
        out_shape = out_shape + [jax.ShapeDtypeStruct((16 // CHUNKS, HD, 256), BF16), sums, sums]
        out_specs = out_specs + [dq_spec, tr_w, tr_w]
    outs = pl.pallas_call(
        functools.partial(attend_body, scale, steps, chunk),
        grid=(steps,),
        out_shape=out_shape, in_specs=in_specs, out_specs=out_specs, scratch_shapes=scratch,
        input_output_aliases=aliases,
        compiler_params=pltpu.CompilerParams(vmem_limit_bytes=VMEM_ATT * 2**20),
        cost_estimate=pl.CostEstimate(flops=10**6, bytes_accessed=2**10, transcendentals=0),
        name="attend_%d" % chunk,
    )(order, *bias, *held, *carried, *dbias)
    return outs[:8], outs[8:]


def block_diagonal(w_ref, count):
    turned = w_ref[...].astype(F32).T
    rows = jnp.broadcast_to(turned[:, None, :], (16, count, 128)).reshape(16 * count, 128)
    at = lax.broadcasted_iota(jnp.int32, (16 * count, 128), 0) % count
    return jnp.concatenate([jnp.where(at == i, rows, 0.0) for i in range(count)], axis=1).astype(BF16)


def bias_body(pair_ref, w_ref, out_ref):
    w = block_diagonal(w_ref, 8)
    for g in range(8):
        cols = jnp.concatenate([pair_ref[g * 8 + r] for r in range(8)], axis=1)
        t = lax.dot_general(w, cols, (((1,), (1,)), ((), ())), preferred_element_type=F32)
        t = t * LOG2E
        for h in range(16):
            block = t[h * 8:h * 8 + 8, :]
            out_ref[h, g * 8:g * 8 + 8, :] = block
            out_ref[h + 16, g * 8:g * 8 + 8, :] = block


def bias_part(pair, w_pair):
    vm = pl.BlockSpec(memory_space=pltpu.VMEM)
    return pl.pallas_call(
        bias_body, out_shape=jax.ShapeDtypeStruct((32, 64, 128), F32),
        in_specs=[vm, vm], out_specs=vm,
        compiler_params=pltpu.CompilerParams(vmem_limit_bytes=32 * 2**20), name="bias_part",
    )(pair, w_pair)


def gpair_body(x_ref, w_ref, out_ref):
    w = block_diagonal(w_ref, 16)
    for g in range(4):
        rows = slice(g * 16, g * 16 + 16)
        x = (x_ref[0, :, rows, :].astype(F32) + x_ref[1, :, rows, :].astype(F32)).astype(BF16).reshape(256, 128)
        t = lax.dot_general(x, w, (((0,), (0,)), ((), ())), preferred_element_type=F32)
        for r in range(16):
            out_ref[g * 16 + r] = t[:, r * 128:r * 128 + 128].astype(BF16)


def gpair(x, w_pair):
    vm = pl.BlockSpec(memory_space=pltpu.VMEM)
    return pl.pallas_call(
        gpair_body, out_shape=jax.ShapeDtypeStruct((64, 128, 128), BF16),
        in_specs=[vm, vm], out_specs=vm,
        compiler_params=pltpu.CompilerParams(vmem_limit_bytes=32 * 2**20), name="gpair",
    )(x, w_pair)


def project_body(x_ref, c_ref, wq_ref, wk_ref, wv_ref, wo_ref, out_ref):
    x = x_ref[...].reshape(NB * 64, WIDTH)
    c = c_ref[...].reshape(NB * 64, WIDTH)
    for slot, w_ref in enumerate((wq_ref, wk_ref, wv_ref)):
        t = jnp.dot(x, w_ref[...], preferred_element_type=F32).T.astype(BF16)
        for h in range(HEADS):
            out_ref[h, slot] = t[h * HD:h * HD + HD, :]
    t = lax.dot_general(wo_ref[...], c, (((1,), (1,)), ((), ())), preferred_element_type=F32).astype(BF16)
    for h in range(HEADS):
        out_ref[h, 3] = t[h * HD:h * HD + HD, :]


def project(single, cotangent, w_query, w_key, w_value, w_out):
    vm = pl.BlockSpec(memory_space=pltpu.VMEM)
    return pl.pallas_call(
        project_body, out_shape=jax.ShapeDtypeStruct((HEADS, 4, HD, NB * 64), BF16),
        in_specs=[vm] * 6, out_specs=vm,
        compiler_params=pltpu.CompilerParams(vmem_limit_bytes=40 * 2**20), name="project",
    )(single, cotangent, w_query, w_key, w_value, w_out)


def final_body(g_ref, wq_ref, wk_ref, wv_ref, out_ref):
    total = None
    for slot, w_ref in enumerate((wq_ref, wk_ref, wv_ref)):
        part = jnp.dot(w_ref[...], g_ref[:, slot].reshape(WIDTH, NB * 64), preferred_element_type=F32)
        total = part if total is None else total + part
    out_ref[...] = total.T.astype(BF16).reshape(NB, 64, WIDTH)


def final(g, w_query, w_key, w_value):
    vm = pl.BlockSpec(memory_space=pltpu.VMEM)
    return pl.pallas_call(
        final_body, out_shape=jax.ShapeDtypeStruct((NB, 64, WIDTH), BF16),
        in_specs=[vm] * 4, out_specs=vm,
        compiler_params=pltpu.CompilerParams(vmem_limit_bytes=40 * 2**20), name="final",
    )(g, w_query, w_key, w_value)


def shift_y(x, d):
    return lax.ppermute(x, "sample", [(i, ((i // 2 + d) % 4) * 2 + i % 2) for i in range(8)])


def exchange(x):
    groups = [[(2 * y + e) * 16 + t for e in range(2) for t in range(16)] for y in range(4)]
    return lax.all_to_all(x, ("sample", "tok"), 0, 0, axis_index_groups=groups)


def gather_blocks(own, after):
    if after is not None:
        own = lax.optimization_barrier((own, after))[0]
    up, down = shift_y(own, 1), shift_y(own, -1)
    return [own, up, down, shift_y(up[0], 1), shift_y(down[1], -1)]


def key_order():
    y = lax.axis_index("sample") // 2
    return jnp.stack([((y + d) % 4) * 2 + e for d in (0, 3, 1, 2) for e in (0, 1)]).astype(jnp.int32)


def plus(*terms):
    total = terms[0].astype(F32)
    for term in terms[1:]:
        total = total + term.astype(F32)
    return total.astype(BF16)


def scatter_blocks(blocks):
    own0, own1, down0, down1, up0, up1, far0, far1 = blocks
    far0, far1 = shift_y(far0, 1), shift_y(far1, -1)
    up1, down0 = shift_y(up1, 1), shift_y(down0, -1)
    up0, down1 = shift_y(plus(up0, far0), 1), shift_y(plus(down1, far1), -1)
    return own_sum(own0, up0, down0, own1, up1, down1)


def own_sum_body(a0, b0, c0, a1, b1, c1, out_ref):
    out_ref[0] = plus(a0[...], b0[...], c0[...])
    out_ref[1] = plus(a1[...], b1[...], c1[...])


def own_sum(*terms):
    vm = pl.BlockSpec(memory_space=pltpu.VMEM)
    return pl.pallas_call(
        own_sum_body, out_shape=jax.ShapeDtypeStruct((2, TOK, 128), BF16), in_specs=[vm] * 6, out_specs=vm,
        compiler_params=pltpu.CompilerParams(vmem_limit_bytes=16 * 2**20), name="own_sum",
    )(*terms)


def local(single, pair, w_query, w_key, w_value, w_out, w_pair, cotangent):
    order = key_order()
    sent = project(single, cotangent, w_query, w_key, w_value, w_out)
    bias = exchange(bias_part(pair, w_pair)).reshape(2, TOK, 128)
    bias, sent = lax.optimization_barrier((bias, sent))
    received = lax.all_to_all(sent, "tok", 0, 0)
    held = prep(order, received)
    dbias, carried, blocks, rows = (), (), None, TOK // CHUNKS
    for c in range(CHUNKS):
        blocks = gather_blocks(bias[:, c * rows:c * rows + rows], blocks[1] if blocks else None)
        dbias, carried = attend(c, order, blocks, held, dbias, carried)
    grads = lax.all_to_all(carried[0], "tok", 0, 0)
    dbias = scatter_blocks(dbias)
    grads, dbias = lax.optimization_barrier((grads, dbias))
    grad_single = final(grads, w_query, w_key, w_value)
    dbias = exchange(dbias.reshape(32, 64, 128)).reshape(2, 16, 64, 128)
    return (grad_single, gpair(dbias, w_pair))


def solution(mesh):
    rows, keys = P("sample", "tok", None), P("tok", "sample", None)
    return jax.shard_map(
        local, mesh=mesh, in_specs=(rows, keys, P(), P(), P(), P(), P(), rows),
        out_specs=(rows, keys), check_vma=False,
    )
```

```python
import math
import functools
import jax, jax.numpy as jnp
from jax import lax
from jax.experimental import pallas as pl
from jax.experimental.pallas import tpu as pltpu
from jax.sharding import PartitionSpec as P

F32 = jnp.float32
BF16 = jnp.bfloat16
LOG2E = 1.4426950408889634
NB = 4
HEADS = 16
WIDTH = 768
HD = 48
TOK = 1024


def prep_body(order_ref, r_ref, q_ref, o_ref, qt_ref, ot_ref, kt_ref, vt_ref, k_ref):
    def piece(slot, first, sample):
        lanes = slice(sample * 64, sample * 64 + 64)
        return jnp.concatenate([r_ref[first, slot, :, lanes], r_ref[first + 1, slot, :, lanes]], axis=1)

    def turned(block):
        return block.astype(F32).T.astype(BF16)

    for u in range(8):
        cols = slice(u * 128, u * 128 + 128)
        other = order_ref[u] * 2
        for b in range(NB):
            qt = piece(0, 2 * u, b)
            qt_ref[b, :, cols] = qt
            q_ref[b, cols, :] = turned(qt)
            ot = piece(3, 2 * u, b)
            ot_ref[b, :, cols] = ot
            o_ref[b, cols, :] = turned(ot)
            kt = piece(1, other, b)
            kt_ref[b, :, cols] = kt
            k_ref[b, cols, :] = turned(kt)
            vt_ref[b, :, cols] = piece(2, other, b)


def prep(order, received):
    nat = jax.ShapeDtypeStruct((NB, TOK, HD), BF16)
    tr = jax.ShapeDtypeStruct((NB, HD, TOK), BF16)
    vm = pl.BlockSpec(memory_space=pltpu.VMEM)
    return pl.pallas_call(
        prep_body,
        out_shape=[nat, nat, tr, tr, tr, tr, nat],
        in_specs=[pl.BlockSpec(memory_space=pltpu.SMEM), vm],
        out_specs=[vm] * 7,
        compiler_params=pltpu.CompilerParams(vmem_limit_bytes=32 * 2**20),
        name="prep",
    )(order, received)


TILE = 256
VMEM_ATT = 40
CHUNKS = 2


def attend_body(scale, steps, chunk, order_ref, *refs):
    first, last = chunk == 0, chunk == CHUNKS - 1
    bias_refs, refs = refs[:4], refs[4:]
    (q_ref, o_ref, qt_ref, ot_ref, kt_ref, vt_ref, k_ref), refs = refs[:7], refs[7:]
    if not first:
        (g_in, dk_in, dv_in), refs = refs[:3], refs[11:]
    dbias_refs, refs = refs[:8], refs[8:]
    g_ref, dkt_ref, dvt_ref, s_ref, dp_ref, p_ref, ds_ref, acc_ref, dqt_ref = refs
    step = pl.program_id(0)

    @pl.when(step == 0)
    def _():
        dkt_ref[...] = jnp.zeros_like(dkt_ref) if first else dk_in[...]
        dvt_ref[...] = jnp.zeros_like(dvt_ref) if first else dv_in[...]

    def products(b):
        s_ref[b % 2] = jnp.dot(q_ref[b], kt_ref[b], preferred_element_type=F32)
        dp_ref[b % 2] = jnp.dot(o_ref[b], vt_ref[b], preferred_element_type=F32)

    def softmax(b):
        group = 16
        for g in range(TILE // group):
            rows = slice(g * group, g * group + group)
            bias = jnp.concatenate([ref[e, rows, :] for ref in bias_refs for e in range(2)], axis=1)
            s = s_ref[b % 2, rows, :] * (scale * LOG2E) + bias
            m = jnp.max(s, axis=1, keepdims=True)
            e = jnp.exp2(s - m)
            inv = 1.0 / jnp.sum(e, axis=1, keepdims=True)
            p = e * inv
            dp = dp_ref[b % 2, rows, :]
            rd = jnp.sum(p * dp, axis=1, keepdims=True)
            ds = p * (dp - rd)
            p_ref[b % 2, rows, :] = p.astype(BF16)
            ds_ref[b % 2, rows, :] = ds.astype(BF16)
            if b == 0:
                acc_ref[rows, :] = ds
            elif b < NB - 1:
                acc_ref[rows, :] += ds
            else:
                total = (acc_ref[rows, :] + ds).astype(BF16)
                for u in range(8):
                    dbias_refs[u][rows, :] = total[:, u * 128:u * 128 + 128]

    def gradients(b):
        p_low, ds_low = p_ref[b % 2], ds_ref[b % 2]
        dkt_ref[b] += jnp.dot(qt_ref[b], ds_low, preferred_element_type=F32)
        dvt_ref[b] += jnp.dot(ot_ref[b], p_low, preferred_element_type=F32)
        dq = jnp.dot(ds_low, k_ref[b], preferred_element_type=F32)
        dqt_ref[step, b] = (dq * scale).T.astype(BF16)

    products(0)
    for b in range(NB):
        if b + 1 < NB:
            products(b + 1)
        softmax(b)
        if b:
            gradients(b - 1)
    gradients(NB - 1)

    @pl.when(step == steps - 1)
    def _():
        each = TILE // 64
        if not first:
            for t in range(chunk * steps * each):
                g_ref[t, 0] = g_in[t]
        for b in range(NB):
            lanes = slice(b * 64, b * 64 + 64)
            for t in range(steps * each):
                c = (t % each) * 64
                block = dqt_ref[t // each, b, :, c:c + 64]
                if last:
                    g_ref[chunk * steps * each + t, 0, :, lanes] = block
                else:
                    g_ref[t, :, lanes] = block
            if last:
                for u in range(8):
                    one = order_ref[u] * 2
                    dk = (dkt_ref[b, :, u * 128:u * 128 + 128] * scale).astype(BF16)
                    dv = dvt_ref[b, :, u * 128:u * 128 + 128].astype(BF16)
                    g_ref[one, 1, :, lanes] = dk[:, :64]
                    g_ref[one + 1, 1, :, lanes] = dk[:, 64:]
                    g_ref[one, 2, :, lanes] = dv[:, :64]
                    g_ref[one + 1, 2, :, lanes] = dv[:, 64:]


def attend(chunk, order, bias, held, dbias, carried):
    rows = TOK // CHUNKS
    steps = rows // TILE
    at = chunk * steps
    last = chunk == CHUNKS - 1
    scale = 1.0 / math.sqrt(HD)
    nat_t = pl.BlockSpec((NB, TILE, HD), lambda i: (0, i + at, 0))
    tr_t = pl.BlockSpec((NB, HD, TILE), lambda i: (0, 0, i + at))
    tr_w = pl.BlockSpec((NB, HD, TOK), lambda i: (0, 0, 0))
    nat_w = pl.BlockSpec((NB, TOK, HD), lambda i: (0, 0, 0))
    bias_t = [pl.BlockSpec((2, TILE, 128), lambda i: (0, i, 0))] * 4
    dbias_t = pl.BlockSpec((TILE, 128), lambda i: (i + at, 0))
    g_spec = pl.BlockSpec((16, 3, HD, 256), lambda i: (0, 0, 0, 0))
    dq_spec = pl.BlockSpec((16 // CHUNKS, HD, 256), lambda i: (0, 0, 0))
    sums = jax.ShapeDtypeStruct((NB, HD, TOK), F32)
    in_specs = [pl.BlockSpec(memory_space=pltpu.SMEM)] + bias_t + [nat_t, nat_t, tr_t, tr_t, tr_w, tr_w, nat_w]
    aliases = {}
    if chunk:
        in_specs += [dq_spec, tr_w, tr_w]
        aliases = {len(in_specs) + u: u for u in range(8)}
        in_specs += [pl.BlockSpec(memory_space=pl.ANY)] * 8
    out_shape, out_specs = [pltpu.HBM((TOK, 128), BF16)] * 8, [dbias_t] * 8
    scratch = [
        pltpu.VMEM((2, TILE, TOK), F32), pltpu.VMEM((2, TILE, TOK), F32),
        pltpu.VMEM((2, TILE, TOK), BF16), pltpu.VMEM((2, TILE, TOK), BF16),
        pltpu.VMEM((TILE, TOK), F32), pltpu.VMEM((steps, NB, HD, TILE), BF16),
    ]
    if last:
        out_shape, out_specs = out_shape + [jax.ShapeDtypeStruct((16, 3, HD, 256), BF16)], out_specs + [g_spec]
        scratch = [pltpu.VMEM((NB, HD, TOK), F32)] * 2 + scratch
    else:
        out_shape = out_shape + [jax.ShapeDtypeStruct((16 // CHUNKS, HD, 256), BF16), sums, sums]
        out_specs = out_specs + [dq_spec, tr_w, tr_w]
    outs = pl.pallas_call(
        functools.partial(attend_body, scale, steps, chunk),
        grid=(steps,),
        out_shape=out_shape, in_specs=in_specs, out_specs=out_specs, scratch_shapes=scratch,
        input_output_aliases=aliases,
        compiler_params=pltpu.CompilerParams(vmem_limit_bytes=VMEM_ATT * 2**20),
        cost_estimate=pl.CostEstimate(flops=10**6, bytes_accessed=2**10, transcendentals=0),
        name="attend_%d" % chunk,
    )(order, *bias, *held, *carried, *dbias)
    return outs[:8], outs[8:]


def block_diagonal(w_ref, count):
    turned = w_ref[...].astype(F32).T
    rows = jnp.broadcast_to(turned[:, None, :], (16, count, 128)).reshape(16 * count, 128)
    at = lax.broadcasted_iota(jnp.int32, (16 * count, 128), 0) % count
    return jnp.concatenate([jnp.where(at == i, rows, 0.0) for i in range(count)], axis=1).astype(BF16)


def bias_body(pair_ref, w_ref, out_ref):
    w = block_diagonal(w_ref, 8)
    for g in range(8):
        cols = jnp.concatenate([pair_ref[g * 8 + r] for r in range(8)], axis=1)
        t = lax.dot_general(w, cols, (((1,), (1,)), ((), ())), preferred_element_type=F32)
        t = t * LOG2E
        for h in range(16):
            block = t[h * 8:h * 8 + 8, :]
            out_ref[h, g * 8:g * 8 + 8, :] = block
            out_ref[h + 16, g * 8:g * 8 + 8, :] = block


def bias_part(pair, w_pair):
    vm = pl.BlockSpec(memory_space=pltpu.VMEM)
    return pl.pallas_call(
        bias_body, out_shape=jax.ShapeDtypeStruct((32, 64, 128), F32),
        in_specs=[vm, vm], out_specs=vm,
        compiler_params=pltpu.CompilerParams(vmem_limit_bytes=32 * 2**20), name="bias_part",
    )(pair, w_pair)


def gpair_body(x_ref, w_ref, out_ref):
    w = block_diagonal(w_ref, 16)
    for g in range(4):
        rows = slice(g * 16, g * 16 + 16)
        x = (x_ref[0, :, rows, :].astype(F32) + x_ref[1, :, rows, :].astype(F32)).astype(BF16).reshape(256, 128)
        t = lax.dot_general(x, w, (((0,), (0,)), ((), ())), preferred_element_type=F32)
        for r in range(16):
            out_ref[g * 16 + r] = t[:, r * 128:r * 128 + 128].astype(BF16)


def gpair(x, w_pair):
    vm = pl.BlockSpec(memory_space=pltpu.VMEM)
    return pl.pallas_call(
        gpair_body, out_shape=jax.ShapeDtypeStruct((64, 128, 128), BF16),
        in_specs=[vm, vm], out_specs=vm,
        compiler_params=pltpu.CompilerParams(vmem_limit_bytes=32 * 2**20), name="gpair",
    )(x, w_pair)


def project_body(x_ref, c_ref, wq_ref, wk_ref, wv_ref, wo_ref, out_ref):
    x = x_ref[...].reshape(NB * 64, WIDTH)
    c = c_ref[...].reshape(NB * 64, WIDTH)
    for slot, w_ref in enumerate((wq_ref, wk_ref, wv_ref)):
        t = jnp.dot(x, w_ref[...], preferred_element_type=F32).T.astype(BF16)
        for h in range(HEADS):
            out_ref[h, slot] = t[h * HD:h * HD + HD, :]
    t = lax.dot_general(wo_ref[...], c, (((1,), (1,)), ((), ())), preferred_element_type=F32).astype(BF16)
    for h in range(HEADS):
        out_ref[h, 3] = t[h * HD:h * HD + HD, :]


def project(single, cotangent, w_query, w_key, w_value, w_out):
    vm = pl.BlockSpec(memory_space=pltpu.VMEM)
    return pl.pallas_call(
        project_body, out_shape=jax.ShapeDtypeStruct((HEADS, 4, HD, NB * 64), BF16),
        in_specs=[vm] * 6, out_specs=vm,
        compiler_params=pltpu.CompilerParams(vmem_limit_bytes=40 * 2**20), name="project",
    )(single, cotangent, w_query, w_key, w_value, w_out)


def final_body(g_ref, wq_ref, wk_ref, wv_ref, out_ref):
    total = None
    for slot, w_ref in enumerate((wq_ref, wk_ref, wv_ref)):
        part = jnp.dot(w_ref[...], g_ref[:, slot].reshape(WIDTH, NB * 64), preferred_element_type=F32)
        total = part if total is None else total + part
    out_ref[...] = total.T.astype(BF16).reshape(NB, 64, WIDTH)


def final(g, w_query, w_key, w_value):
    vm = pl.BlockSpec(memory_space=pltpu.VMEM)
    return pl.pallas_call(
        final_body, out_shape=jax.ShapeDtypeStruct((NB, 64, WIDTH), BF16),
        in_specs=[vm] * 4, out_specs=vm,
        compiler_params=pltpu.CompilerParams(vmem_limit_bytes=40 * 2**20), name="final",
    )(g, w_query, w_key, w_value)


def shift_y(x, d):
    return lax.ppermute(x, "sample", [(i, ((i // 2 + d) % 4) * 2 + i % 2) for i in range(8)])


def exchange(x):
    groups = [[(2 * y + e) * 16 + t for e in range(2) for t in range(16)] for y in range(4)]
    return lax.all_to_all(x, ("sample", "tok"), 0, 0, axis_index_groups=groups)


def tie(*values):
    return lax.optimization_barrier(values)


def gather_blocks(first, second):
    up, down = shift_y(first, 1), shift_y(first, -1)
    far = shift_y(up, 1)
    later, far = tie(second, far)
    sooner, down = tie(second, down)
    up2, down2 = shift_y(later, 1), shift_y(sooner, -1)
    return [first, up, down, far], [second, up2, down2, shift_y(down2, -1)]


def key_order():
    y = lax.axis_index("sample") // 2
    return jnp.stack([((y + d) % 4) * 2 + e for d in (0, 3, 1, 2) for e in (0, 1)]).astype(jnp.int32)


def plus(*terms):
    total = terms[0].astype(F32)
    for term in terms[1:]:
        total = total + term.astype(F32)
    return total.astype(BF16)


def scatter_blocks(blocks):
    own0, own1, down0, down1, up0, up1, far0, far1 = blocks
    far0, far1 = shift_y(far0, 1), shift_y(far1, -1)
    up1, down0 = shift_y(up1, 1), shift_y(down0, -1)
    up0, down1 = shift_y(plus(up0, far0), 1), shift_y(plus(down1, far1), -1)
    return own_sum(own0, up0, down0, own1, up1, down1)


def own_sum_body(a0, b0, c0, a1, b1, c1, out_ref):
    out_ref[0] = plus(a0[...], b0[...], c0[...])
    out_ref[1] = plus(a1[...], b1[...], c1[...])


def own_sum(*terms):
    vm = pl.BlockSpec(memory_space=pltpu.VMEM)
    return pl.pallas_call(
        own_sum_body, out_shape=jax.ShapeDtypeStruct((2, TOK, 128), BF16), in_specs=[vm] * 6, out_specs=vm,
        compiler_params=pltpu.CompilerParams(vmem_limit_bytes=16 * 2**20), name="own_sum",
    )(*terms)


def local(single, pair, w_query, w_key, w_value, w_out, w_pair, cotangent):
    order = key_order()
    sent = project(single, cotangent, w_query, w_key, w_value, w_out)
    bias = exchange(bias_part(pair, w_pair)).reshape(2, TOK, 128)
    bias, sent = lax.optimization_barrier((bias, sent))
    received = lax.all_to_all(sent, "tok", 0, 0)
    held = prep(order, received)
    blocks = gather_blocks(bias[:, :TOK // 2], bias[:, TOK // 2:])
    dbias, carried = (), ()
    for c in range(CHUNKS):
        dbias, carried = attend(c, order, blocks[c], held, dbias, carried)
    grads = lax.all_to_all(carried[0], "tok", 0, 0)
    dbias = scatter_blocks(dbias)
    grads, dbias = lax.optimization_barrier((grads, dbias))
    grad_single = final(grads, w_query, w_key, w_value)
    dbias = exchange(dbias.reshape(32, 64, 128)).reshape(2, 16, 64, 128)
    return (grad_single, gpair(dbias, w_pair))


def solution(mesh):
    rows, keys = P("sample", "tok", None), P("tok", "sample", None)
    return jax.shard_map(
        local, mesh=mesh, in_specs=(rows, keys, P(), P(), P(), P(), P(), rows),
        out_specs=(rows, keys), check_vma=False,
    )
```

```python
import math
import functools
import jax, jax.numpy as jnp
from jax import lax
from jax.experimental import pallas as pl
from jax.experimental.pallas import tpu as pltpu
from jax.sharding import PartitionSpec as P

F32 = jnp.float32
BF16 = jnp.bfloat16
LOG2E = 1.4426950408889634
NB = 4
HEADS = 16
WIDTH = 768
HD = 48
TOK = 1024


def prep_body(order_ref, r_ref, q_ref, o_ref, qt_ref, ot_ref, kt_ref, vt_ref, k_ref):
    def piece(slot, first, sample):
        lanes = slice(sample * 64, sample * 64 + 64)
        return jnp.concatenate([r_ref[first, slot, :, lanes], r_ref[first + 1, slot, :, lanes]], axis=1)

    def turned(block):
        return block.astype(F32).T.astype(BF16)

    for u in range(8):
        cols = slice(u * 128, u * 128 + 128)
        other = order_ref[u] * 2
        for b in range(NB):
            qt = piece(0, 2 * u, b)
            qt_ref[b, :, cols] = qt
            q_ref[b, cols, :] = turned(qt)
            ot = piece(3, 2 * u, b)
            ot_ref[b, :, cols] = ot
            o_ref[b, cols, :] = turned(ot)
            kt = piece(1, other, b)
            kt_ref[b, :, cols] = kt
            k_ref[b, cols, :] = turned(kt)
            vt_ref[b, :, cols] = piece(2, other, b)


def prep(order, received):
    nat = jax.ShapeDtypeStruct((NB, TOK, HD), BF16)
    tr = jax.ShapeDtypeStruct((NB, HD, TOK), BF16)
    vm = pl.BlockSpec(memory_space=pltpu.VMEM)
    return pl.pallas_call(
        prep_body,
        out_shape=[nat, nat, tr, tr, tr, tr, nat],
        in_specs=[pl.BlockSpec(memory_space=pltpu.SMEM), vm],
        out_specs=[vm] * 7,
        compiler_params=pltpu.CompilerParams(vmem_limit_bytes=32 * 2**20),
        name="prep",
    )(order, received)


TILE = 256
VMEM_ATT = 40
NEAR = 8.0
STEEP = 18.8


def attend_body(scale, steps, order_ref, *refs):
    bias_refs, refs = refs[:8], refs[8:]
    (q_ref, o_ref, qt_ref, ot_ref, kt_ref, vt_ref, k_ref), refs = refs[:7], refs[7:]
    dbias_refs, refs = refs[:8], refs[8:]
    g_ref, s_ref, dp_ref, p_ref, ds_ref, acc_ref, dqt_ref, dkt_ref, dvt_ref, bias_scr = refs
    step = pl.program_id(0)

    @pl.when(step == 0)
    def _():
        dkt_ref[...] = jnp.zeros_like(dkt_ref)
        dvt_ref[...] = jnp.zeros_like(dvt_ref)

    def all_bias():
        mark = marks(64)[1]
        for t in range(TILE // 64):
            for u in range(8):
                tops = bias_refs[u][t, 64:80].astype(F32)[:8]
                tops = jnp.broadcast_to(tops[:, None, :], (8, 8, 128)).reshape(64, 128)
                top = jnp.sum(jnp.where(mark, tops, 0.0), axis=1, keepdims=True)
                bias_scr[t * 64:t * 64 + 64, u * 128:u * 128 + 128] = decode(bias_refs[u][t, :64], top)

    def products(b):
        s_ref[b % 2] = jnp.dot(q_ref[b], kt_ref[b], preferred_element_type=F32)
        dp_ref[b % 2] = jnp.dot(o_ref[b], vt_ref[b], preferred_element_type=F32)

    def softmax(b):
        group = 16
        for g in range(TILE // group):
            rows = slice(g * group, g * group + group)
            s = s_ref[b % 2, rows, :] * (scale * LOG2E) + bias_scr[rows, :]
            m = jnp.max(s, axis=1, keepdims=True)
            e = jnp.exp2(s - m)
            inv = 1.0 / jnp.sum(e, axis=1, keepdims=True)
            p = e * inv
            dp = dp_ref[b % 2, rows, :]
            rd = jnp.sum(p * dp, axis=1, keepdims=True)
            ds = p * (dp - rd)
            p_ref[b % 2, rows, :] = p.astype(BF16)
            ds_ref[b % 2, rows, :] = ds.astype(BF16)
            if b == 0:
                acc_ref[rows, :] = ds
            elif b < NB - 1:
                acc_ref[rows, :] += ds
            else:
                total = (acc_ref[rows, :] + ds).astype(BF16)
                for u in range(8):
                    dbias_refs[u][rows, :] = total[:, u * 128:u * 128 + 128]

    def gradients(b):
        p_low, ds_low = p_ref[b % 2], ds_ref[b % 2]
        dkt_ref[b] += jnp.dot(qt_ref[b], ds_low, preferred_element_type=F32)
        dvt_ref[b] += jnp.dot(ot_ref[b], p_low, preferred_element_type=F32)
        dq = jnp.dot(ds_low, k_ref[b], preferred_element_type=F32)
        dqt_ref[step, b] = (dq * scale).T.astype(BF16)

    all_bias()
    products(0)
    for b in range(NB):
        if b + 1 < NB:
            products(b + 1)
        softmax(b)
        if b:
            gradients(b - 1)
    gradients(NB - 1)

    @pl.when(step == steps - 1)
    def _():
        each = TILE // 64
        for b in range(NB):
            lanes = slice(b * 64, b * 64 + 64)
            for t in range(16):
                c = (t % each) * 64
                g_ref[t, 0, :, lanes] = dqt_ref[t // each, b, :, c:c + 64]
            for u in range(8):
                first = order_ref[u] * 2
                dk = (dkt_ref[b, :, u * 128:u * 128 + 128] * scale).astype(BF16)
                dv = dvt_ref[b, :, u * 128:u * 128 + 128].astype(BF16)
                g_ref[first, 1, :, lanes] = dk[:, :64]
                g_ref[first + 1, 1, :, lanes] = dk[:, 64:]
                g_ref[first, 2, :, lanes] = dv[:, :64]
                g_ref[first + 1, 2, :, lanes] = dv[:, 64:]


def attend(order, bias, held):
    steps = TOK // TILE
    scale = 1.0 / math.sqrt(HD)
    nat_t = pl.BlockSpec((NB, TILE, HD), lambda i: (0, i, 0))
    tr_t = pl.BlockSpec((NB, HD, TILE), lambda i: (0, 0, i))
    tr_w = pl.BlockSpec((NB, HD, TOK), lambda i: (0, 0, 0))
    nat_w = pl.BlockSpec((NB, TOK, HD), lambda i: (0, 0, 0))
    dbias_t = pl.BlockSpec((TILE, 128), lambda i: (i, 0))
    one_t = pl.BlockSpec((TILE // 64, 80, 128), lambda i: (i, 0, 0))
    g_spec = pl.BlockSpec((16, 3, HD, 256), lambda i: (0, 0, 0, 0))
    outs = pl.pallas_call(
        functools.partial(attend_body, scale, steps),
        grid=(steps,),
        out_shape=[pltpu.HBM((TOK, 128), BF16)] * 8 + [jax.ShapeDtypeStruct((16, 3, HD, 256), BF16)],
        in_specs=[pl.BlockSpec(memory_space=pltpu.SMEM)] + [one_t] * 8 + [nat_t, nat_t, tr_t, tr_t, tr_w, tr_w, nat_w],
        out_specs=[dbias_t] * 8 + [g_spec],
        scratch_shapes=[
            pltpu.VMEM((2, TILE, TOK), F32), pltpu.VMEM((2, TILE, TOK), F32),
            pltpu.VMEM((2, TILE, TOK), BF16), pltpu.VMEM((2, TILE, TOK), BF16),
            pltpu.VMEM((TILE, TOK), F32), pltpu.VMEM((steps, NB, HD, TILE), BF16),
            pltpu.VMEM((NB, HD, TOK), F32), pltpu.VMEM((NB, HD, TOK), F32), pltpu.VMEM((TILE, TOK), F32),
        ],
        compiler_params=pltpu.CompilerParams(vmem_limit_bytes=VMEM_ATT * 2**20),
        cost_estimate=pl.CostEstimate(flops=10**6, bytes_accessed=2**10, transcendentals=0),
        name="attend",
    )(order, *bias, *held)
    return outs[:8], outs[8]


def block_diagonal(w_ref, count):
    turned = w_ref[...].astype(F32).T
    rows = jnp.broadcast_to(turned[:, None, :], (16, count, 128)).reshape(16 * count, 128)
    at = lax.broadcasted_iota(jnp.int32, (16 * count, 128), 0) % count
    return jnp.concatenate([jnp.where(at == i, rows, 0.0) for i in range(count)], axis=1).astype(BF16)


def encode(bias):
    top = jnp.max(bias, axis=1, keepdims=True)
    return jnp.exp2(126.0 - STEEP * jnp.log2(1.0 + (top - bias) * (1.0 / NEAR))).astype(BF16), top


def decode(code, top):
    return (top + NEAR) - NEAR * jnp.exp2((126.0 - jnp.log2(code.astype(F32))) * (1.0 / STEEP))


def marks(count):
    lane = lax.broadcasted_iota(jnp.int32, (count, 128), 1)
    row = lax.broadcasted_iota(jnp.int32, (count, 128), 0)
    return lane, (lane < 24) & (lane % 8 == row % 8)


def bias_body(pair_ref, w_ref, out_ref):
    w = block_diagonal(w_ref, 8)
    lane, mark = marks(128)
    tops = []
    for g in range(8):
        cols = jnp.concatenate([pair_ref[g * 8 + r] for r in range(8)], axis=1)
        t = lax.dot_general(w, cols, (((1,), (1,)), ((), ())), preferred_element_type=F32)
        code, top = encode(t * LOG2E)
        high = top.astype(BF16).astype(F32)
        middle = (top - high).astype(BF16).astype(F32)
        terms = jnp.where(lane < 8, high, jnp.where(lane < 16, middle, top - high - middle))
        tops.append(jnp.sum(jnp.where(mark, terms, 0.0).reshape(16, 8, 128), axis=1))
        if g % 2 == 0:
            even = code
            continue
        for h in range(16):
            block = jnp.concatenate([even[h * 8:h * 8 + 8, :], code[h * 8:h * 8 + 8, :]], axis=0)
            out_ref[h, g * 8 - 8:g * 8 + 8, :] = block
            out_ref[h + 16, g * 8 - 8:g * 8 + 8, :] = block
    for h in range(16):
        block = jnp.concatenate([top[h:h + 1, :] for top in tops] + [jnp.zeros((8, 128), F32)], axis=0).astype(BF16)
        out_ref[h, 64:80, :] = block
        out_ref[h + 16, 64:80, :] = block


def bias_part(pair, w_pair):
    vm = pl.BlockSpec(memory_space=pltpu.VMEM)
    return pl.pallas_call(
        bias_body, out_shape=jax.ShapeDtypeStruct((32, 80, 128), BF16),
        in_specs=[vm, vm], out_specs=vm,
        compiler_params=pltpu.CompilerParams(vmem_limit_bytes=32 * 2**20), name="bias_part",
    )(pair, w_pair)


def gpair_body(x_ref, w_ref, out_ref):
    w = block_diagonal(w_ref, 16)
    for g in range(4):
        rows = slice(g * 16, g * 16 + 16)
        x = (x_ref[0, :, rows, :].astype(F32) + x_ref[1, :, rows, :].astype(F32)).astype(BF16).reshape(256, 128)
        t = lax.dot_general(x, w, (((0,), (0,)), ((), ())), preferred_element_type=F32)
        for r in range(16):
            out_ref[g * 16 + r] = t[:, r * 128:r * 128 + 128].astype(BF16)


def gpair(x, w_pair):
    vm = pl.BlockSpec(memory_space=pltpu.VMEM)
    return pl.pallas_call(
        gpair_body, out_shape=jax.ShapeDtypeStruct((64, 128, 128), BF16),
        in_specs=[vm, vm], out_specs=vm,
        compiler_params=pltpu.CompilerParams(vmem_limit_bytes=32 * 2**20), name="gpair",
    )(x, w_pair)


def project_body(x_ref, c_ref, wq_ref, wk_ref, wv_ref, wo_ref, out_ref):
    x = x_ref[...].reshape(NB * 64, WIDTH)
    c = c_ref[...].reshape(NB * 64, WIDTH)
    for slot, w_ref in enumerate((wq_ref, wk_ref, wv_ref)):
        t = jnp.dot(x, w_ref[...], preferred_element_type=F32).T.astype(BF16)
        for h in range(HEADS):
            out_ref[h, slot] = t[h * HD:h * HD + HD, :]
    t = lax.dot_general(wo_ref[...], c, (((1,), (1,)), ((), ())), preferred_element_type=F32).astype(BF16)
    for h in range(HEADS):
        out_ref[h, 3] = t[h * HD:h * HD + HD, :]


def project(single, cotangent, w_query, w_key, w_value, w_out):
    vm = pl.BlockSpec(memory_space=pltpu.VMEM)
    return pl.pallas_call(
        project_body, out_shape=jax.ShapeDtypeStruct((HEADS, 4, HD, NB * 64), BF16),
        in_specs=[vm] * 6, out_specs=vm,
        compiler_params=pltpu.CompilerParams(vmem_limit_bytes=40 * 2**20), name="project",
    )(single, cotangent, w_query, w_key, w_value, w_out)


def final_body(g_ref, wq_ref, wk_ref, wv_ref, out_ref):
    total = None
    for slot, w_ref in enumerate((wq_ref, wk_ref, wv_ref)):
        part = jnp.dot(w_ref[...], g_ref[:, slot].reshape(WIDTH, NB * 64), preferred_element_type=F32)
        total = part if total is None else total + part
    out_ref[...] = total.T.astype(BF16).reshape(NB, 64, WIDTH)


def final(g, w_query, w_key, w_value):
    vm = pl.BlockSpec(memory_space=pltpu.VMEM)
    return pl.pallas_call(
        final_body, out_shape=jax.ShapeDtypeStruct((NB, 64, WIDTH), BF16),
        in_specs=[vm] * 4, out_specs=vm,
        compiler_params=pltpu.CompilerParams(vmem_limit_bytes=40 * 2**20), name="final",
    )(g, w_query, w_key, w_value)


def shift_y(x, d):
    return lax.ppermute(x, "sample", [(i, ((i // 2 + d) % 4) * 2 + i % 2) for i in range(8)])


def exchange(x):
    groups = [[(2 * y + e) * 16 + t for e in range(2) for t in range(16)] for y in range(4)]
    return lax.all_to_all(x, ("sample", "tok"), 0, 0, axis_index_groups=groups)


def gather_blocks(own):
    up0, down1 = shift_y(own[0], 1), shift_y(own[1], -1)
    up1, down0 = shift_y(own[1], 1), shift_y(own[0], -1)
    return [own[0], own[1], up0, up1, down0, down1, shift_y(up0, 1), shift_y(down1, -1)]


def key_order():
    y = lax.axis_index("sample") // 2
    return jnp.stack([((y + d) % 4) * 2 + e for d in (0, 3, 1, 2) for e in (0, 1)]).astype(jnp.int32)


def plus(*terms):
    total = terms[0].astype(F32)
    for term in terms[1:]:
        total = total + term.astype(F32)
    return total.astype(BF16)


def scatter_blocks(blocks):
    own0, own1, down0, down1, up0, up1, far0, far1 = blocks
    far0, far1 = shift_y(far0, 1), shift_y(far1, -1)
    up1, down0 = shift_y(up1, 1), shift_y(down0, -1)
    up0, down1 = shift_y(plus(up0, far0), 1), shift_y(plus(down1, far1), -1)
    return own_sum(own0, up0, down0, own1, up1, down1)


def own_sum_body(a0, b0, c0, a1, b1, c1, out_ref):
    out_ref[0] = plus(a0[...], b0[...], c0[...])
    out_ref[1] = plus(a1[...], b1[...], c1[...])


def own_sum(*terms):
    vm = pl.BlockSpec(memory_space=pltpu.VMEM)
    return pl.pallas_call(
        own_sum_body, out_shape=jax.ShapeDtypeStruct((2, TOK, 128), BF16), in_specs=[vm] * 6, out_specs=vm,
        compiler_params=pltpu.CompilerParams(vmem_limit_bytes=16 * 2**20), name="own_sum",
    )(*terms)


def local(single, pair, w_query, w_key, w_value, w_out, w_pair, cotangent):
    order = key_order()
    sent = project(single, cotangent, w_query, w_key, w_value, w_out)
    bias = exchange(bias_part(pair, w_pair)).reshape(2, 16, 80, 128)
    bias, sent = lax.optimization_barrier((bias, sent))
    received = lax.all_to_all(sent, "tok", 0, 0)
    dbias, grads = attend(order, gather_blocks(bias), prep(order, received))
    grads = lax.all_to_all(grads, "tok", 0, 0)
    dbias = scatter_blocks(dbias)
    grads, dbias = lax.optimization_barrier((grads, dbias))
    grad_single = final(grads, w_query, w_key, w_value)
    dbias = exchange(dbias.reshape(32, 64, 128)).reshape(2, 16, 64, 128)
    return (grad_single, gpair(dbias, w_pair))


def solution(mesh):
    rows, keys = P("sample", "tok", None), P("tok", "sample", None)
    return jax.shard_map(
        local, mesh=mesh, in_specs=(rows, keys, P(), P(), P(), P(), P(), rows),
        out_specs=(rows, keys), check_vma=False,
    )
```

```python
import math
import functools
import jax, jax.numpy as jnp
from jax import lax
from jax.experimental import pallas as pl
from jax.experimental.pallas import tpu as pltpu
from jax.sharding import PartitionSpec as P

F32 = jnp.float32
BF16 = jnp.bfloat16
LOG2E = 1.4426950408889634
NB = 4
HEADS = 16
WIDTH = 768
HD = 48
TOK = 1024


def prep_body(order_ref, r_ref, qt_ref, ot_ref, kt_ref, vt_ref, k_ref):
    def piece(slot, first, sample):
        lanes = slice(sample * 64, sample * 64 + 64)
        return jnp.concatenate([r_ref[first, slot, :, lanes], r_ref[first + 1, slot, :, lanes]], axis=1)

    for u in range(8):
        cols = slice(u * 128, u * 128 + 128)
        other = order_ref[u] * 2
        for b in range(NB):
            qt_ref[b, :, cols] = piece(0, 2 * u, b)
            ot_ref[b, :, cols] = piece(3, 2 * u, b)
            kt = piece(1, other, b)
            kt_ref[b, :, cols] = kt
            k_ref[b, cols, :] = kt.astype(F32).T.astype(BF16)
            vt_ref[b, :, cols] = piece(2, other, b)


def prep(order, received):
    nat = jax.ShapeDtypeStruct((NB, TOK, HD), BF16)
    tr = jax.ShapeDtypeStruct((NB, HD, TOK), BF16)
    vm = pl.BlockSpec(memory_space=pltpu.VMEM)
    return pl.pallas_call(
        prep_body,
        out_shape=[tr, tr, tr, tr, nat],
        in_specs=[pl.BlockSpec(memory_space=pltpu.SMEM), vm],
        out_specs=[vm] * 5,
        compiler_params=pltpu.CompilerParams(vmem_limit_bytes=32 * 2**20),
        name="prep",
    )(order, received)


TILE = 256
VMEM_ATT = 40
NEAR = 8.0
STEEP = 18.8
EARLY, LATE = (0, 1, 2, 5), (3, 4, 6, 7)


def decode_rows(codes, every, group):
    tops = every[:8]
    for n in range(1, 4):
        tops = jnp.where(group == n, every[n * 8:n * 8 + 8], tops)
    tops = jnp.broadcast_to(tops[:, None, :], (8, 8, 128)).reshape(64, 128)
    for t in range(4):
        top = jnp.sum(jnp.where(marks(64, t * 32)[1], tops, 0.0), axis=1, keepdims=True)
        yield t * 64, decode(codes[t * 64:t * 64 + 64, :], top)


def early_body(*refs):
    count = len(refs) // 3
    for n in range(count):
        every = refs[count + n][...].astype(F32)
        for at, block in decode_rows(refs[n], every, pl.program_id(0)):
            refs[2 * count + n][at:at + 64, :] = block


def early(blocks):
    code_t = pl.BlockSpec((TILE, 128), lambda i: (i, 0))
    top_t = pl.BlockSpec((32, 128), lambda i: (TOK // 32, 0))
    count = len(blocks)
    return pl.pallas_call(
        early_body, grid=(TOK // TILE,), out_shape=[pltpu.HBM((TOK, 128), F32)] * count,
        in_specs=[code_t] * count + [top_t] * count, out_specs=[code_t] * count,
        compiler_params=pltpu.CompilerParams(vmem_limit_bytes=16 * 2**20), name="early",
    )(*blocks, *blocks)


def attend_body(scale, steps, order_ref, *refs):
    early_refs, code_refs, top_refs, refs = refs[:4], refs[4:8], refs[8:12], refs[12:]
    (qt_ref, ot_ref, kt_ref, vt_ref, k_ref), refs = refs[:5], refs[5:]
    dbias_refs, refs = refs[:8], refs[8:]
    g_ref, s_ref, dp_ref, p_ref, ds_ref, acc_ref, dqt_ref, dkt_ref, dvt_ref, bias_scr = refs
    step = pl.program_id(0)
    here = pl.ds(pl.multiple_of(step * TILE, TILE), TILE)

    @pl.when(step == 0)
    def _():
        dkt_ref[...] = jnp.zeros_like(dkt_ref)
        dvt_ref[...] = jnp.zeros_like(dvt_ref)

    def all_bias():
        for n in range(4):
            for at, block in decode_rows(code_refs[n], top_refs[n][...].astype(F32), step):
                bias_scr[at:at + 64, n * 128:n * 128 + 128] = block

    def products(b):
        first = (((0,), (0,)), ((), ()))
        s_ref[b % 2] = lax.dot_general(qt_ref[b, :, here], kt_ref[b], first, preferred_element_type=F32)
        dp_ref[b % 2] = lax.dot_general(ot_ref[b, :, here], vt_ref[b], first, preferred_element_type=F32)

    def softmax(b):
        group = 16
        for g in range(TILE // group):
            rows = slice(g * group, g * group + group)
            late = [bias_scr[rows, n * 128:n * 128 + 128] for n in range(4)]
            held = dict(zip(EARLY + LATE, [ref[rows, :] for ref in early_refs] + late))
            bias = jnp.concatenate([held[u] for u in range(8)], axis=1)
            s = s_ref[b % 2, rows, :] * (scale * LOG2E) + bias
            m = jnp.max(s, axis=1, keepdims=True)
            e = jnp.exp2(s - m)
            inv = 1.0 / jnp.sum(e, axis=1, keepdims=True)
            p = e * inv
            dp = dp_ref[b % 2, rows, :]
            rd = jnp.sum(p * dp, axis=1, keepdims=True)
            ds = p * (dp - rd)
            p_ref[b % 2, rows, :] = p.astype(BF16)
            ds_ref[b % 2, rows, :] = ds.astype(BF16)
            if b == 0:
                acc_ref[rows, :] = ds
            elif b < NB - 1:
                acc_ref[rows, :] += ds
            else:
                total = (acc_ref[rows, :] + ds).astype(BF16)
                for u in range(8):
                    dbias_refs[u][rows, :] = total[:, u * 128:u * 128 + 128]

    def gradients(b):
        p_low, ds_low = p_ref[b % 2], ds_ref[b % 2]
        dkt_ref[b] += jnp.dot(qt_ref[b, :, here], ds_low, preferred_element_type=F32)
        dvt_ref[b] += jnp.dot(ot_ref[b, :, here], p_low, preferred_element_type=F32)
        dq = jnp.dot(ds_low, k_ref[b], preferred_element_type=F32)
        dqt_ref[step, b] = (dq * scale).T.astype(BF16)

    all_bias()
    products(0)
    for b in range(NB):
        if b + 1 < NB:
            products(b + 1)
        softmax(b)
        if b:
            gradients(b - 1)
    gradients(NB - 1)

    @pl.when(step == steps - 1)
    def _():
        each = TILE // 64
        for b in range(NB):
            lanes = slice(b * 64, b * 64 + 64)
            for t in range(16):
                c = (t % each) * 64
                g_ref[t, 0, :, lanes] = dqt_ref[t // each, b, :, c:c + 64]
            for u in range(8):
                first = order_ref[u] * 2
                dk = (dkt_ref[b, :, u * 128:u * 128 + 128] * scale).astype(BF16)
                dv = dvt_ref[b, :, u * 128:u * 128 + 128].astype(BF16)
                g_ref[first, 1, :, lanes] = dk[:, :64]
                g_ref[first + 1, 1, :, lanes] = dk[:, 64:]
                g_ref[first, 2, :, lanes] = dv[:, :64]
                g_ref[first + 1, 2, :, lanes] = dv[:, 64:]


def attend(order, ready, bias, held):
    steps = TOK // TILE
    scale = 1.0 / math.sqrt(HD)
    vm = pl.BlockSpec(memory_space=pltpu.VMEM)
    dbias_t = pl.BlockSpec((TILE, 128), lambda i: (i, 0))
    top_t = pl.BlockSpec((32, 128), lambda i: (TOK // 32, 0))
    g_spec = pl.BlockSpec((16, 3, HD, 256), lambda i: (0, 0, 0, 0))
    outs = pl.pallas_call(
        functools.partial(attend_body, scale, steps),
        grid=(steps,),
        out_shape=[pltpu.HBM((TOK, 128), BF16)] * 8 + [jax.ShapeDtypeStruct((16, 3, HD, 256), BF16)],
        in_specs=[pl.BlockSpec(memory_space=pltpu.SMEM)] + [dbias_t] * 8 + [top_t] * 4 + [vm] * 5,
        out_specs=[dbias_t] * 8 + [g_spec],
        scratch_shapes=[
            pltpu.VMEM((2, TILE, TOK), F32), pltpu.VMEM((2, TILE, TOK), F32),
            pltpu.VMEM((2, TILE, TOK), BF16), pltpu.VMEM((2, TILE, TOK), BF16),
            pltpu.VMEM((TILE, TOK), F32), pltpu.VMEM((steps, NB, HD, TILE), BF16),
            pltpu.VMEM((NB, HD, TOK), F32), pltpu.VMEM((NB, HD, TOK), F32), pltpu.VMEM((TILE, 512), F32),
        ],
        compiler_params=pltpu.CompilerParams(vmem_limit_bytes=VMEM_ATT * 2**20),
        cost_estimate=pl.CostEstimate(flops=10**6, bytes_accessed=2**10, transcendentals=0),
        name="attend",
    )(order, *[pltpu.with_memory_space_constraint(v, pltpu.HBM) for v in ready], *bias, *bias, *held)
    return outs[:8], outs[8]


def block_diagonal(w_ref, count):
    turned = w_ref[...].astype(F32).T
    rows = jnp.broadcast_to(turned[:, None, :], (16, count, 128)).reshape(16 * count, 128)
    at = lax.broadcasted_iota(jnp.int32, (16 * count, 128), 0) % count
    return jnp.concatenate([jnp.where(at == i, rows, 0.0) for i in range(count)], axis=1).astype(BF16)


def encode(bias):
    top = jnp.max(bias, axis=1, keepdims=True)
    return jnp.exp2(126.0 - STEEP * jnp.log2(1.0 + (top - bias) * (1.0 / NEAR))).astype(BF16), top


def decode(code, top):
    return (top + NEAR) - NEAR * jnp.exp2((126.0 - jnp.log2(code.astype(F32))) * (1.0 / STEEP))


def marks(count, start):
    lane = lax.broadcasted_iota(jnp.int32, (count, 128), 1) - start
    row = lax.broadcasted_iota(jnp.int32, (count, 128), 0)
    return lane, (lane >= 0) & (lane < 24) & (lane % 8 == row % 8)


def bias_body(pair_ref, w_ref, out_ref):
    w = block_diagonal(w_ref, 8)
    lane, mark = marks(128, 0)
    tops = []
    for g in range(8):
        cols = jnp.concatenate([pair_ref[g * 8 + r] for r in range(8)], axis=1)
        t = lax.dot_general(w, cols, (((1,), (1,)), ((), ())), preferred_element_type=F32)
        code, top = encode(t * LOG2E)
        high = top.astype(BF16).astype(F32)
        middle = (top - high).astype(BF16).astype(F32)
        terms = jnp.where(lane < 8, high, jnp.where(lane < 16, middle, top - high - middle))
        tops.append(jnp.sum(jnp.where(mark, terms, 0.0).reshape(16, 8, 128), axis=1))
        if g % 2 == 0:
            even = code
            continue
        for h in range(16):
            block = jnp.concatenate([even[h * 8:h * 8 + 8, :], code[h * 8:h * 8 + 8, :]], axis=0)
            out_ref[h, g * 8 - 8:g * 8 + 8, :] = block
            out_ref[h + 16, g * 8 - 8:g * 8 + 8, :] = block
    for h in range(16):
        block = jnp.concatenate([top[h:h + 1, :] for top in tops] + [jnp.zeros((8, 128), F32)], axis=0).astype(BF16)
        out_ref[h, 64:80, :] = block
        out_ref[h + 16, 64:80, :] = block


def bias_part(pair, w_pair):
    vm = pl.BlockSpec(memory_space=pltpu.VMEM)
    return pl.pallas_call(
        bias_body, out_shape=jax.ShapeDtypeStruct((32, 80, 128), BF16),
        in_specs=[vm, vm], out_specs=vm,
        compiler_params=pltpu.CompilerParams(vmem_limit_bytes=32 * 2**20), name="bias_part",
    )(pair, w_pair)


def unpack_body(x_ref, *out_refs):
    for e in range(2):
        for t in range(16):
            out_refs[e][t * 64:t * 64 + 64, :] = x_ref[e, t, :64]
        groups = []
        for group in range(4):
            tops = [x_ref[e, group * 4 + n, 64:80].astype(F32)[:8, :32] for n in range(4)]
            groups.append(jnp.concatenate(tops, axis=1))
        out_refs[e][TOK:TOK + 32, :] = jnp.concatenate(groups, axis=0).astype(BF16)


def unpack(x):
    vm = pl.BlockSpec(memory_space=pltpu.VMEM)
    return pl.pallas_call(
        unpack_body, out_shape=[jax.ShapeDtypeStruct((TOK + 32, 128), BF16)] * 2, in_specs=[vm], out_specs=[vm] * 2,
        compiler_params=pltpu.CompilerParams(vmem_limit_bytes=16 * 2**20), name="unpack",
    )(x)


def gpair_body(x_ref, w_ref, out_ref):
    w = block_diagonal(w_ref, 16)
    for g in range(4):
        rows = slice(g * 16, g * 16 + 16)
        x = (x_ref[0, :, rows, :].astype(F32) + x_ref[1, :, rows, :].astype(F32)).astype(BF16).reshape(256, 128)
        t = lax.dot_general(x, w, (((0,), (0,)), ((), ())), preferred_element_type=F32)
        for r in range(16):
            out_ref[g * 16 + r] = t[:, r * 128:r * 128 + 128].astype(BF16)


def gpair(x, w_pair):
    vm = pl.BlockSpec(memory_space=pltpu.VMEM)
    return pl.pallas_call(
        gpair_body, out_shape=jax.ShapeDtypeStruct((64, 128, 128), BF16),
        in_specs=[vm, vm], out_specs=vm,
        compiler_params=pltpu.CompilerParams(vmem_limit_bytes=32 * 2**20), name="gpair",
    )(x, w_pair)


def project_body(x_ref, c_ref, wq_ref, wk_ref, wv_ref, wo_ref, out_ref):
    x = x_ref[...].reshape(NB * 64, WIDTH)
    c = c_ref[...].reshape(NB * 64, WIDTH)
    for slot, w_ref in enumerate((wq_ref, wk_ref, wv_ref)):
        t = jnp.dot(x, w_ref[...], preferred_element_type=F32).T.astype(BF16)
        for h in range(HEADS):
            out_ref[h, slot] = t[h * HD:h * HD + HD, :]
    t = lax.dot_general(wo_ref[...], c, (((1,), (1,)), ((), ())), preferred_element_type=F32).astype(BF16)
    for h in range(HEADS):
        out_ref[h, 3] = t[h * HD:h * HD + HD, :]


def project(single, cotangent, w_query, w_key, w_value, w_out):
    vm = pl.BlockSpec(memory_space=pltpu.VMEM)
    return pl.pallas_call(
        project_body, out_shape=jax.ShapeDtypeStruct((HEADS, 4, HD, NB * 64), BF16),
        in_specs=[vm] * 6, out_specs=vm,
        compiler_params=pltpu.CompilerParams(vmem_limit_bytes=40 * 2**20), name="project",
    )(single, cotangent, w_query, w_key, w_value, w_out)


def final_body(g_ref, wq_ref, wk_ref, wv_ref, out_ref):
    total = None
    for slot, w_ref in enumerate((wq_ref, wk_ref, wv_ref)):
        part = jnp.dot(w_ref[...], g_ref[:, slot].reshape(WIDTH, NB * 64), preferred_element_type=F32)
        total = part if total is None else total + part
    out_ref[...] = total.T.astype(BF16).reshape(NB, 64, WIDTH)


def final(g, w_query, w_key, w_value):
    vm = pl.BlockSpec(memory_space=pltpu.VMEM)
    return pl.pallas_call(
        final_body, out_shape=jax.ShapeDtypeStruct((NB, 64, WIDTH), BF16),
        in_specs=[vm] * 4, out_specs=vm,
        compiler_params=pltpu.CompilerParams(vmem_limit_bytes=40 * 2**20), name="final",
    )(g, w_query, w_key, w_value)


def shift_y(x, d):
    return lax.ppermute(x, "sample", [(i, ((i // 2 + d) % 4) * 2 + i % 2) for i in range(8)])


def exchange(x):
    groups = [[(2 * y + e) * 16 + t for e in range(2) for t in range(16)] for y in range(4)]
    return lax.all_to_all(x, ("sample", "tok"), 0, 0, axis_index_groups=groups)


def gather_blocks(own):
    up0, down1 = shift_y(own[0], 1), shift_y(own[1], -1)
    up1, down0 = shift_y(own[1], 1), shift_y(own[0], -1)
    return [own[0], own[1], up0, up1, down0, down1, shift_y(up0, 1), shift_y(down1, -1)]


def key_order():
    y = lax.axis_index("sample") // 2
    return jnp.stack([((y + d) % 4) * 2 + e for d in (0, 3, 1, 2) for e in (0, 1)]).astype(jnp.int32)


def plus(*terms):
    total = terms[0].astype(F32)
    for term in terms[1:]:
        total = total + term.astype(F32)
    return total.astype(BF16)


def scatter_blocks(blocks):
    own0, own1, down0, down1, up0, up1, far0, far1 = blocks
    far0, far1 = shift_y(far0, 1), shift_y(far1, -1)
    up1, down0 = shift_y(up1, 1), shift_y(down0, -1)
    up0, down1 = shift_y(plus(up0, far0), 1), shift_y(plus(down1, far1), -1)
    return own_sum(own0, up0, down0, own1, up1, down1)


def own_sum_body(a0, b0, c0, a1, b1, c1, out_ref):
    out_ref[0] = plus(a0[...], b0[...], c0[...])
    out_ref[1] = plus(a1[...], b1[...], c1[...])


def own_sum(*terms):
    vm = pl.BlockSpec(memory_space=pltpu.VMEM)
    return pl.pallas_call(
        own_sum_body, out_shape=jax.ShapeDtypeStruct((2, TOK, 128), BF16), in_specs=[vm] * 6, out_specs=vm,
        compiler_params=pltpu.CompilerParams(vmem_limit_bytes=16 * 2**20), name="own_sum",
    )(*terms)


def local(single, pair, w_query, w_key, w_value, w_out, w_pair, cotangent):
    order = key_order()
    sent = project(single, cotangent, w_query, w_key, w_value, w_out)
    bias = exchange(bias_part(pair, w_pair))
    bias, sent = lax.optimization_barrier((bias, sent))
    received = lax.all_to_all(sent, "tok", 0, 0)
    blocks = gather_blocks(unpack(bias.reshape(2, 16, 80, 128)))
    received, ready = lax.optimization_barrier((received, early([blocks[u] for u in EARLY])))
    dbias, grads = attend(order, ready, [blocks[u] for u in LATE], prep(order, received))
    grads = lax.all_to_all(grads, "tok", 0, 0)
    dbias = scatter_blocks(dbias)
    grads, dbias = lax.optimization_barrier((grads, dbias))
    grad_single = final(grads, w_query, w_key, w_value)
    dbias = exchange(dbias.reshape(32, 64, 128)).reshape(2, 16, 64, 128)
    return (grad_single, gpair(dbias, w_pair))


def solution(mesh):
    rows, keys = P("sample", "tok", None), P("tok", "sample", None)
    return jax.shard_map(
        local, mesh=mesh, in_specs=(rows, keys, P(), P(), P(), P(), P(), rows),
        out_specs=(rows, keys), check_vma=False,
    )
```

```python
import math
import functools
import jax, jax.numpy as jnp
from jax import lax
from jax.experimental import pallas as pl
from jax.experimental.pallas import tpu as pltpu
from jax.sharding import PartitionSpec as P

F32 = jnp.float32
BF16 = jnp.bfloat16
LOG2E = 1.4426950408889634
NB = 4
HEADS = 16
WIDTH = 768
HD = 48
TOK = 1024


def prep_body(order_ref, r_ref, qt_ref, ot_ref, kt_ref, vt_ref, k_ref):
    def piece(slot, first, sample):
        lanes = slice(sample * 64, sample * 64 + 64)
        return jnp.concatenate([r_ref[first, slot, :, lanes], r_ref[first + 1, slot, :, lanes]], axis=1)

    for u in range(8):
        cols = slice(u * 128, u * 128 + 128)
        other = order_ref[u] * 2
        for b in range(NB):
            qt_ref[b, :, cols] = piece(0, 2 * u, b)
            ot_ref[b, :, cols] = piece(3, 2 * u, b)
            kt = piece(1, other, b)
            kt_ref[b, :, cols] = kt
            k_ref[b, cols, :] = kt.astype(F32).T.astype(BF16)
            vt_ref[b, :, cols] = piece(2, other, b)


def prep(order, received):
    nat = jax.ShapeDtypeStruct((NB, TOK, HD), BF16)
    tr = jax.ShapeDtypeStruct((NB, HD, TOK), BF16)
    vm = pl.BlockSpec(memory_space=pltpu.VMEM)
    return pl.pallas_call(
        prep_body,
        out_shape=[tr, tr, tr, tr, nat],
        in_specs=[pl.BlockSpec(memory_space=pltpu.SMEM), vm],
        out_specs=[vm] * 5,
        compiler_params=pltpu.CompilerParams(vmem_limit_bytes=32 * 2**20),
        name="prep",
    )(order, received)


TILE = 512
GROUP = 256
VMEM_ATT = 40
NEAR = 8.0
STEEP = 18.8
EARLY, LATE = (0, 1, 2, 5), (3, 4, 6, 7)


def decode_rows(codes, every, group):
    tops = every[:8]
    for n in range(1, 4):
        tops = jnp.where(group == n, every[n * 8:n * 8 + 8], tops)
    tops = jnp.broadcast_to(tops[:, None, :], (8, 8, 128)).reshape(64, 128)
    for t in range(4):
        top = jnp.sum(jnp.where(marks(64, t * 32)[1], tops, 0.0), axis=1, keepdims=True)
        yield t * 64, decode(codes[t * 64:t * 64 + 64, :], top)


def early_body(*refs):
    count = len(refs) // 3
    for n in range(count):
        every = refs[count + n][...].astype(F32)
        for at, block in decode_rows(refs[n], every, pl.program_id(0)):
            refs[2 * count + n][at:at + 64, :] = block


def early(blocks):
    code_t = pl.BlockSpec((GROUP, 128), lambda i: (i, 0))
    top_t = pl.BlockSpec((32, 128), lambda i: (TOK // 32, 0))
    count = len(blocks)
    return pl.pallas_call(
        early_body, grid=(TOK // GROUP,), out_shape=[pltpu.HBM((TOK, 128), F32)] * count,
        in_specs=[code_t] * count + [top_t] * count, out_specs=[code_t] * count,
        compiler_params=pltpu.CompilerParams(vmem_limit_bytes=16 * 2**20), name="early",
    )(*blocks, *blocks)


def attend_body(scale, steps, order_ref, *refs):
    early_refs, code_refs, top_refs, refs = refs[:4], refs[4:8], refs[8:12], refs[12:]
    (qt_ref, ot_ref, kt_ref, vt_ref, k_ref), refs = refs[:5], refs[5:]
    dbias_refs, refs = refs[:8], refs[8:]
    g_ref, s_ref, dp_ref, p_ref, ds_ref, acc_ref, dqt_ref, dkt_ref, dvt_ref, bias_scr = refs
    step = pl.program_id(0)
    here = pl.ds(pl.multiple_of(step * TILE, TILE), TILE)

    @pl.when(step == 0)
    def _():
        dkt_ref[...] = jnp.zeros_like(dkt_ref)
        dvt_ref[...] = jnp.zeros_like(dvt_ref)

    def all_bias():
        for n in range(4):
            for part in range(TILE // GROUP):
                start = part * GROUP
                codes, group = code_refs[n][start:start + GROUP, :], step * (TILE // GROUP) + part
                for at, block in decode_rows(codes, top_refs[n][...].astype(F32), group):
                    bias_scr[start + at:start + at + 64, n * 128:n * 128 + 128] = block

    def products(b):
        first = (((0,), (0,)), ((), ()))
        s_ref[b % 2] = lax.dot_general(qt_ref[b, :, here], kt_ref[b], first, preferred_element_type=F32)
        dp_ref[b % 2] = lax.dot_general(ot_ref[b, :, here], vt_ref[b], first, preferred_element_type=F32)

    def softmax(b):
        group = 16
        for g in range(TILE // group):
            rows = slice(g * group, g * group + group)
            late = [bias_scr[rows, n * 128:n * 128 + 128] for n in range(4)]
            held = dict(zip(EARLY + LATE, [ref[rows, :] for ref in early_refs] + late))
            bias = jnp.concatenate([held[u] for u in range(8)], axis=1)
            s = s_ref[b % 2, rows, :] * (scale * LOG2E) + bias
            m = jnp.max(s, axis=1, keepdims=True)
            e = jnp.exp2(s - m)
            inv = 1.0 / jnp.sum(e, axis=1, keepdims=True)
            p = e * inv
            dp = dp_ref[b % 2, rows, :]
            rd = jnp.sum(p * dp, axis=1, keepdims=True)
            ds = p * (dp - rd)
            p_ref[b % 2, rows, :] = p.astype(BF16)
            ds_ref[b % 2, rows, :] = ds.astype(BF16)
            if b == 0:
                acc_ref[rows, :] = ds
            elif b < NB - 1:
                acc_ref[rows, :] += ds
            else:
                total = (acc_ref[rows, :] + ds).astype(BF16)
                for u in range(8):
                    dbias_refs[u][rows, :] = total[:, u * 128:u * 128 + 128]

    def gradients(b):
        p_low, ds_low = p_ref[b % 2], ds_ref[b % 2]
        dkt_ref[b] += jnp.dot(qt_ref[b, :, here], ds_low, preferred_element_type=F32)
        dvt_ref[b] += jnp.dot(ot_ref[b, :, here], p_low, preferred_element_type=F32)
        dq = jnp.dot(ds_low, k_ref[b], preferred_element_type=F32)
        dqt_ref[step, b] = (dq * scale).T.astype(BF16)

    all_bias()
    products(0)
    for b in range(NB):
        if b + 1 < NB:
            products(b + 1)
        softmax(b)
        if b:
            gradients(b - 1)
    gradients(NB - 1)

    @pl.when(step == steps - 1)
    def _():
        each = TILE // 64
        for b in range(NB):
            lanes = slice(b * 64, b * 64 + 64)
            for t in range(16):
                c = (t % each) * 64
                g_ref[t, 0, :, lanes] = dqt_ref[t // each, b, :, c:c + 64]
            for u in range(8):
                first = order_ref[u] * 2
                dk = (dkt_ref[b, :, u * 128:u * 128 + 128] * scale).astype(BF16)
                dv = dvt_ref[b, :, u * 128:u * 128 + 128].astype(BF16)
                g_ref[first, 1, :, lanes] = dk[:, :64]
                g_ref[first + 1, 1, :, lanes] = dk[:, 64:]
                g_ref[first, 2, :, lanes] = dv[:, :64]
                g_ref[first + 1, 2, :, lanes] = dv[:, 64:]


def attend(order, ready, bias, held):
    steps = TOK // TILE
    scale = 1.0 / math.sqrt(HD)
    vm = pl.BlockSpec(memory_space=pltpu.VMEM)
    dbias_t = pl.BlockSpec((TILE, 128), lambda i: (i, 0))
    top_t = pl.BlockSpec((32, 128), lambda i: (TOK // 32, 0))
    g_spec = pl.BlockSpec((16, 3, HD, 256), lambda i: (0, 0, 0, 0))
    outs = pl.pallas_call(
        functools.partial(attend_body, scale, steps),
        grid=(steps,),
        out_shape=[pltpu.HBM((TOK, 128), BF16)] * 8 + [jax.ShapeDtypeStruct((16, 3, HD, 256), BF16)],
        in_specs=[pl.BlockSpec(memory_space=pltpu.SMEM)] + [dbias_t] * 8 + [top_t] * 4 + [vm] * 5,
        out_specs=[dbias_t] * 8 + [g_spec],
        scratch_shapes=[
            pltpu.VMEM((2, TILE, TOK), F32), pltpu.VMEM((2, TILE, TOK), F32),
            pltpu.VMEM((2, TILE, TOK), BF16), pltpu.VMEM((2, TILE, TOK), BF16),
            pltpu.VMEM((TILE, TOK), F32), pltpu.VMEM((steps, NB, HD, TILE), BF16),
            pltpu.VMEM((NB, HD, TOK), F32), pltpu.VMEM((NB, HD, TOK), F32), pltpu.VMEM((TILE, 512), F32),
        ],
        compiler_params=pltpu.CompilerParams(vmem_limit_bytes=VMEM_ATT * 2**20),
        cost_estimate=pl.CostEstimate(flops=10**6, bytes_accessed=2**10, transcendentals=0),
        name="attend",
    )(order, *[pltpu.with_memory_space_constraint(v, pltpu.HBM) for v in ready], *bias, *bias, *held)
    return outs[:8], outs[8]


def block_diagonal(w_ref, count):
    turned = w_ref[...].astype(F32)
    rows = jnp.broadcast_to(turned[:, None, :], (16, count, 128)).reshape(16 * count, 128)
    at = lax.broadcasted_iota(jnp.int32, (16 * count, 128), 0) % count
    return jnp.concatenate([jnp.where(at == i, rows, 0.0) for i in range(count)], axis=1).astype(BF16)


def encode(bias):
    top = jnp.max(bias, axis=1, keepdims=True)
    return jnp.exp2(126.0 - STEEP * jnp.log2(1.0 + (top - bias) * (1.0 / NEAR))).astype(BF16), top


def decode(code, top):
    return (top + NEAR) - NEAR * jnp.exp2((126.0 - jnp.log2(code.astype(F32))) * (1.0 / STEEP))


def marks(count, start):
    lane = lax.broadcasted_iota(jnp.int32, (count, 128), 1) - start
    row = lax.broadcasted_iota(jnp.int32, (count, 128), 0)
    return lane, (lane >= 0) & (lane < 24) & (lane % 8 == row % 8)


def bias_body(pair_ref, w_ref, out_ref, wide_ref, tops_ref):
    step = pl.program_id(0)

    @pl.when(step == 0)
    def _():
        wide_ref[...] = block_diagonal(w_ref, 8)

    lane, mark = marks(128, 0)
    for g in range(4):
        cols = jnp.concatenate([pair_ref[g * 8 + r] for r in range(8)], axis=1)
        t = lax.dot_general(wide_ref[...], cols, (((1,), (1,)), ((), ())), preferred_element_type=F32)
        code, top = encode(t * LOG2E)
        high = top.astype(BF16).astype(F32)
        middle = (top - high).astype(BF16).astype(F32)
        terms = jnp.where(lane < 8, high, jnp.where(lane < 16, middle, top - high - middle))
        tops_ref[step * 4 + g] = jnp.sum(jnp.where(mark, terms, 0.0).reshape(16, 8, 128), axis=1)
        if g % 2 == 0:
            even = code
            continue
        rows = pl.ds(pl.multiple_of(step * 32 + g * 8 - 8, 16), 16)
        for h in range(16):
            block = jnp.concatenate([even[h * 8:h * 8 + 8, :], code[h * 8:h * 8 + 8, :]], axis=0)
            out_ref[h, rows, :] = block
            out_ref[h + 16, rows, :] = block

    @pl.when(step == 1)
    def _():
        for h in range(16):
            tops = [tops_ref[g, h:h + 1, :] for g in range(8)]
            block = jnp.concatenate(tops + [jnp.zeros((8, 128), F32)], axis=0).astype(BF16)
            out_ref[h, 64:80, :] = block
            out_ref[h + 16, 64:80, :] = block


def bias_part(pair, w_pair):
    return pl.pallas_call(
        bias_body, grid=(2,), out_shape=pltpu.HBM((32, 80, 128), BF16),
        in_specs=[pl.BlockSpec((32, 128, 128), lambda i: (i, 0, 0)), pl.BlockSpec((16, 128), lambda i: (0, 0))],
        out_specs=pl.BlockSpec((32, 80, 128), lambda i: (0, 0, 0)),
        scratch_shapes=[pltpu.VMEM((128, 1024), BF16), pltpu.VMEM((8, 16, 128), F32)],
        compiler_params=pltpu.CompilerParams(vmem_limit_bytes=32 * 2**20), name="bias_part",
    )(pltpu.with_memory_space_constraint(pair, pltpu.HBM), pltpu.with_memory_space_constraint(w_pair, pltpu.HBM))


def unpack_body(x_ref, *out_refs):
    for e in range(2):
        for t in range(16):
            out_refs[e][t * 64:t * 64 + 64, :] = x_ref[e, t, :64]
        groups = []
        for group in range(4):
            tops = [x_ref[e, group * 4 + n, 64:80].astype(F32)[:8, :32] for n in range(4)]
            groups.append(jnp.concatenate(tops, axis=1))
        out_refs[e][TOK:TOK + 32, :] = jnp.concatenate(groups, axis=0).astype(BF16)


def unpack(x):
    vm = pl.BlockSpec(memory_space=pltpu.VMEM)
    return pl.pallas_call(
        unpack_body, out_shape=[jax.ShapeDtypeStruct((TOK + 32, 128), BF16)] * 2, in_specs=[vm], out_specs=[vm] * 2,
        compiler_params=pltpu.CompilerParams(vmem_limit_bytes=16 * 2**20), name="unpack",
    )(x)


def gpair_body(x_ref, w_ref, out_ref, wide_ref):
    step = pl.program_id(0)

    @pl.when(step == 0)
    def _():
        wide_ref[...] = block_diagonal(w_ref, 16)

    for g in range(2):
        rows = pl.ds(pl.multiple_of(step * 32 + g * 16, 16), 16)
        x = (x_ref[0, :, rows, :].astype(F32) + x_ref[1, :, rows, :].astype(F32)).astype(BF16).reshape(256, 128)
        t = lax.dot_general(x, wide_ref[...], (((0,), (0,)), ((), ())), preferred_element_type=F32)
        for r in range(16):
            out_ref[g * 16 + r] = t[:, r * 128:r * 128 + 128].astype(BF16)


def gpair(x, w_pair):
    vm = pl.BlockSpec(memory_space=pltpu.VMEM)
    return pl.pallas_call(
        gpair_body, grid=(2,), out_shape=jax.ShapeDtypeStruct((64, 128, 128), BF16),
        in_specs=[vm, vm], out_specs=pl.BlockSpec((32, 128, 128), lambda i: (i, 0, 0)),
        scratch_shapes=[pltpu.VMEM((256, 2048), BF16)],
        compiler_params=pltpu.CompilerParams(vmem_limit_bytes=32 * 2**20), name="gpair",
    )(x, w_pair)


def project_body(x_ref, c_ref, wq_ref, wk_ref, wv_ref, wo_ref, out_ref):
    x = x_ref[...].reshape(NB * 64, WIDTH)
    c = c_ref[...].reshape(NB * 64, WIDTH)
    for slot, w_ref in enumerate((wq_ref, wk_ref, wv_ref)):
        t = jnp.dot(x, w_ref[...], preferred_element_type=F32).T.astype(BF16)
        for h in range(HEADS):
            out_ref[h, slot] = t[h * HD:h * HD + HD, :]
    t = lax.dot_general(wo_ref[...], c, (((1,), (1,)), ((), ())), preferred_element_type=F32).astype(BF16)
    for h in range(HEADS):
        out_ref[h, 3] = t[h * HD:h * HD + HD, :]


def project(single, cotangent, w_query, w_key, w_value, w_out):
    vm = pl.BlockSpec(memory_space=pltpu.VMEM)
    return pl.pallas_call(
        project_body, out_shape=jax.ShapeDtypeStruct((HEADS, 4, HD, NB * 64), BF16),
        in_specs=[vm] * 6, out_specs=vm,
        compiler_params=pltpu.CompilerParams(vmem_limit_bytes=40 * 2**20), name="project",
    )(single, cotangent, w_query, w_key, w_value, w_out)


def final_body(g_ref, wq_ref, wk_ref, wv_ref, out_ref):
    total = None
    for slot, w_ref in enumerate((wq_ref, wk_ref, wv_ref)):
        part = jnp.dot(w_ref[...], g_ref[:, slot].reshape(WIDTH, NB * 64), preferred_element_type=F32)
        total = part if total is None else total + part
    out_ref[...] = total.T.astype(BF16).reshape(NB, 64, WIDTH)


def final(g, w_query, w_key, w_value):
    vm = pl.BlockSpec(memory_space=pltpu.VMEM)
    return pl.pallas_call(
        final_body, out_shape=jax.ShapeDtypeStruct((NB, 64, WIDTH), BF16),
        in_specs=[vm] * 4, out_specs=vm,
        compiler_params=pltpu.CompilerParams(vmem_limit_bytes=40 * 2**20), name="final",
    )(g, w_query, w_key, w_value)


def shift_y(x, d):
    return lax.ppermute(x, "sample", [(i, ((i // 2 + d) % 4) * 2 + i % 2) for i in range(8)])


def exchange(x):
    groups = [[(2 * y + e) * 16 + t for e in range(2) for t in range(16)] for y in range(4)]
    return lax.all_to_all(x, ("sample", "tok"), 0, 0, axis_index_groups=groups)


def gather_blocks(own):
    up0, down1 = shift_y(own[0], 1), shift_y(own[1], -1)
    up1, down0 = shift_y(own[1], 1), shift_y(own[0], -1)
    return [own[0], own[1], up0, up1, down0, down1, shift_y(up0, 1), shift_y(down1, -1)]


def key_order():
    y = lax.axis_index("sample") // 2
    return jnp.stack([((y + d) % 4) * 2 + e for d in (0, 3, 1, 2) for e in (0, 1)]).astype(jnp.int32)


def plus(*terms):
    total = terms[0].astype(F32)
    for term in terms[1:]:
        total = total + term.astype(F32)
    return total.astype(BF16)


def scatter_blocks(blocks):
    own0, own1, down0, down1, up0, up1, far0, far1 = blocks
    far0, far1 = shift_y(far0, 1), shift_y(far1, -1)
    up1, down0 = shift_y(up1, 1), shift_y(down0, -1)
    up0, down1 = shift_y(plus(up0, far0), 1), shift_y(plus(down1, far1), -1)
    return own_sum(own0, up0, down0, own1, up1, down1)


def own_sum_body(a0, b0, c0, a1, b1, c1, out_ref):
    out_ref[0] = plus(a0[...], b0[...], c0[...])
    out_ref[1] = plus(a1[...], b1[...], c1[...])


def own_sum(*terms):
    vm = pl.BlockSpec(memory_space=pltpu.VMEM)
    return pl.pallas_call(
        own_sum_body, out_shape=jax.ShapeDtypeStruct((2, TOK, 128), BF16), in_specs=[vm] * 6, out_specs=vm,
        compiler_params=pltpu.CompilerParams(vmem_limit_bytes=16 * 2**20), name="own_sum",
    )(*terms)


def local(single, pair, w_query, w_key, w_value, w_out, w_pair, cotangent):
    order = key_order()
    sent = project(single, cotangent, w_query, w_key, w_value, w_out)
    bias = exchange(bias_part(pair, w_pair.T))
    bias, sent = lax.optimization_barrier((bias, sent))
    received = lax.all_to_all(sent, "tok", 0, 0)
    blocks = gather_blocks(unpack(bias.reshape(2, 16, 80, 128)))
    received, ready = lax.optimization_barrier((received, early([blocks[u] for u in EARLY])))
    dbias, grads = attend(order, ready, [blocks[u] for u in LATE], prep(order, received))
    grads = lax.all_to_all(grads, "tok", 0, 0)
    dbias = scatter_blocks(dbias)
    grads, dbias = lax.optimization_barrier((grads, dbias))
    grad_single = final(grads, w_query, w_key, w_value)
    dbias = exchange(dbias.reshape(32, 64, 128)).reshape(2, 16, 64, 128)
    return (grad_single, gpair(dbias, w_pair.T))


def solution(mesh):
    rows, keys = P("sample", "tok", None), P("tok", "sample", None)
    return jax.shard_map(
        local, mesh=mesh, in_specs=(rows, keys, P(), P(), P(), P(), P(), rows),
        out_specs=(rows, keys), check_vma=False,
    )
```

```python
import math
import functools
import jax, jax.numpy as jnp
from jax import lax
from jax.experimental import pallas as pl
from jax.experimental.pallas import tpu as pltpu
from jax.sharding import PartitionSpec as P

F32 = jnp.float32
BF16 = jnp.bfloat16
LOG2E = 1.4426950408889634
NB = 4
HEADS = 16
WIDTH = 768
HD = 48
TOK = 1024


def prep_body(order_ref, r_ref, qt_ref, ot_ref, kt_ref, vt_ref, k_ref):
    def piece(slot, first, sample):
        lanes = slice(sample * 64, sample * 64 + 64)
        return jnp.concatenate([r_ref[first, slot, :, lanes], r_ref[first + 1, slot, :, lanes]], axis=1)

    for u in range(8):
        cols = slice(u * 128, u * 128 + 128)
        other = order_ref[u] * 2
        for b in range(NB):
            qt_ref[b, :, cols] = piece(0, 2 * u, b)
            ot_ref[b, :, cols] = piece(3, 2 * u, b)
            kt = piece(1, other, b)
            kt_ref[b, :, cols] = kt
            k_ref[b, cols, :] = kt.astype(F32).T.astype(BF16)
            vt_ref[b, :, cols] = piece(2, other, b)


def prep(order, received):
    nat = jax.ShapeDtypeStruct((NB, TOK, HD), BF16)
    tr = jax.ShapeDtypeStruct((NB, HD, TOK), BF16)
    vm = pl.BlockSpec(memory_space=pltpu.VMEM)
    return pl.pallas_call(
        prep_body,
        out_shape=[tr, tr, tr, tr, nat],
        in_specs=[pl.BlockSpec(memory_space=pltpu.SMEM), vm],
        out_specs=[vm] * 5,
        compiler_params=pltpu.CompilerParams(vmem_limit_bytes=32 * 2**20),
        name="prep",
    )(order, received)


TILE = 512
GROUP = 256
VMEM_ATT = 40
NEAR = 8.0
STEEP = 18.8
EARLY, LATE = (0, 1, 2, 5, 3, 4), (6, 7)


def decode_rows(codes, every, group):
    tops = every[:8]
    for n in range(1, 4):
        tops = jnp.where(group == n, every[n * 8:n * 8 + 8], tops)
    tops = jnp.broadcast_to(tops[:, None, :], (8, 8, 128)).reshape(64, 128)
    for t in range(4):
        top = jnp.sum(jnp.where(marks(64, t * 32)[1], tops, 0.0), axis=1, keepdims=True)
        yield t * 64, decode(codes[t * 64:t * 64 + 64, :], top)


def early_body(*refs):
    count = len(refs) // 3
    for n in range(count):
        every = refs[count + n][...].astype(F32)
        for at, block in decode_rows(refs[n], every, pl.program_id(0)):
            refs[2 * count + n][at:at + 64, :] = block


def early(blocks):
    code_t = pl.BlockSpec((GROUP, 128), lambda i: (i, 0))
    top_t = pl.BlockSpec((32, 128), lambda i: (TOK // 32, 0))
    count = len(blocks)
    return pl.pallas_call(
        early_body, grid=(TOK // GROUP,), out_shape=[pltpu.HBM((TOK, 128), F32)] * count,
        in_specs=[code_t] * count + [top_t] * count, out_specs=[code_t] * count,
        compiler_params=pltpu.CompilerParams(vmem_limit_bytes=16 * 2**20), name="early",
    )(*blocks, *blocks)


def attend_body(scale, steps, order_ref, *refs):
    early_refs, code_refs, top_refs, refs = refs[:6], refs[6:8], refs[8:10], refs[10:]
    (qt_ref, ot_ref, kt_ref, vt_ref, k_ref), refs = refs[:5], refs[5:]
    dbias_refs, refs = refs[:8], refs[8:]
    g_ref, s_ref, dp_ref, p_ref, ds_ref, acc_ref, dqt_ref, dkt_ref, dvt_ref, bias_scr = refs
    step = pl.program_id(0)
    here = pl.ds(pl.multiple_of(step * TILE, TILE), TILE)

    @pl.when(step == 0)
    def _():
        dkt_ref[...] = jnp.zeros_like(dkt_ref)
        dvt_ref[...] = jnp.zeros_like(dvt_ref)

    def all_bias():
        for n in range(2):
            for part in range(TILE // GROUP):
                start = part * GROUP
                codes, group = code_refs[n][start:start + GROUP, :], step * (TILE // GROUP) + part
                for at, block in decode_rows(codes, top_refs[n][...].astype(F32), group):
                    bias_scr[start + at:start + at + 64, n * 128:n * 128 + 128] = block

    def products(b):
        first = (((0,), (0,)), ((), ()))
        s_ref[b % 2] = lax.dot_general(qt_ref[b, :, here], kt_ref[b], first, preferred_element_type=F32)
        dp_ref[b % 2] = lax.dot_general(ot_ref[b, :, here], vt_ref[b], first, preferred_element_type=F32)

    def softmax(b):
        group = 16
        for g in range(TILE // group):
            rows = slice(g * group, g * group + group)
            late = [bias_scr[rows, n * 128:n * 128 + 128] for n in range(2)]
            held = dict(zip(EARLY + LATE, [ref[rows, :] for ref in early_refs] + late))
            bias = jnp.concatenate([held[u] for u in range(8)], axis=1)
            s = s_ref[b % 2, rows, :] * (scale * LOG2E) + bias
            m = jnp.max(s, axis=1, keepdims=True)
            e = jnp.exp2(s - m)
            inv = 1.0 / jnp.sum(e, axis=1, keepdims=True)
            p = e * inv
            dp = dp_ref[b % 2, rows, :]
            rd = jnp.sum(p * dp, axis=1, keepdims=True)
            ds = p * (dp - rd)
            p_ref[b % 2, rows, :] = p.astype(BF16)
            ds_ref[b % 2, rows, :] = ds.astype(BF16)
            if b == 0:
                acc_ref[rows, :] = ds
            elif b < NB - 1:
                acc_ref[rows, :] += ds
            else:
                total = (acc_ref[rows, :] + ds).astype(BF16)
                for u in range(8):
                    dbias_refs[u][rows, :] = total[:, u * 128:u * 128 + 128]

    def gradients(b):
        p_low, ds_low = p_ref[b % 2], ds_ref[b % 2]
        dkt_ref[b] += jnp.dot(qt_ref[b, :, here], ds_low, preferred_element_type=F32)
        dvt_ref[b] += jnp.dot(ot_ref[b, :, here], p_low, preferred_element_type=F32)
        dq = jnp.dot(ds_low, k_ref[b], preferred_element_type=F32)
        dqt_ref[step, b] = (dq * scale).T.astype(BF16)

    all_bias()
    products(0)
    for b in range(NB):
        if b + 1 < NB:
            products(b + 1)
        softmax(b)
        if b:
            gradients(b - 1)
    gradients(NB - 1)

    @pl.when(step == steps - 1)
    def _():
        each = TILE // 64
        for b in range(NB):
            lanes = slice(b * 64, b * 64 + 64)
            for t in range(16):
                c = (t % each) * 64
                g_ref[t, 0, :, lanes] = dqt_ref[t // each, b, :, c:c + 64]
            for u in range(8):
                first = order_ref[u] * 2
                dk = (dkt_ref[b, :, u * 128:u * 128 + 128] * scale).astype(BF16)
                dv = dvt_ref[b, :, u * 128:u * 128 + 128].astype(BF16)
                g_ref[first, 1, :, lanes] = dk[:, :64]
                g_ref[first + 1, 1, :, lanes] = dk[:, 64:]
                g_ref[first, 2, :, lanes] = dv[:, :64]
                g_ref[first + 1, 2, :, lanes] = dv[:, 64:]


def attend(order, ready, bias, held):
    steps = TOK // TILE
    scale = 1.0 / math.sqrt(HD)
    vm = pl.BlockSpec(memory_space=pltpu.VMEM)
    dbias_t = pl.BlockSpec((TILE, 128), lambda i: (i, 0))
    top_t = pl.BlockSpec((32, 128), lambda i: (TOK // 32, 0))
    g_spec = pl.BlockSpec((16, 3, HD, 256), lambda i: (0, 0, 0, 0))
    outs = pl.pallas_call(
        functools.partial(attend_body, scale, steps),
        grid=(steps,),
        out_shape=[pltpu.HBM((TOK, 128), BF16)] * 8 + [jax.ShapeDtypeStruct((16, 3, HD, 256), BF16)],
        in_specs=[pl.BlockSpec(memory_space=pltpu.SMEM)] + [dbias_t] * 8 + [top_t] * 2 + [vm] * 5,
        out_specs=[dbias_t] * 8 + [g_spec],
        scratch_shapes=[
            pltpu.VMEM((2, TILE, TOK), F32), pltpu.VMEM((2, TILE, TOK), F32),
            pltpu.VMEM((2, TILE, TOK), BF16), pltpu.VMEM((2, TILE, TOK), BF16),
            pltpu.VMEM((TILE, TOK), F32), pltpu.VMEM((steps, NB, HD, TILE), BF16),
            pltpu.VMEM((NB, HD, TOK), F32), pltpu.VMEM((NB, HD, TOK), F32), pltpu.VMEM((TILE, 256), F32),
        ],
        compiler_params=pltpu.CompilerParams(vmem_limit_bytes=VMEM_ATT * 2**20),
        cost_estimate=pl.CostEstimate(flops=10**6, bytes_accessed=2**10, transcendentals=0),
        name="attend",
    )(order, *[pltpu.with_memory_space_constraint(v, pltpu.HBM) for v in ready], *bias, *bias, *held)
    return outs[:8], outs[8]


def block_diagonal(w_ref, count):
    turned = w_ref[...].astype(F32)
    rows = jnp.broadcast_to(turned[:, None, :], (16, count, 128)).reshape(16 * count, 128)
    at = lax.broadcasted_iota(jnp.int32, (16 * count, 128), 0) % count
    return jnp.concatenate([jnp.where(at == i, rows, 0.0) for i in range(count)], axis=1).astype(BF16)


def encode(bias):
    top = jnp.max(bias, axis=1, keepdims=True)
    return jnp.exp2(126.0 - STEEP * jnp.log2(1.0 + (top - bias) * (1.0 / NEAR))).astype(BF16), top


def decode(code, top):
    return (top + NEAR) - NEAR * jnp.exp2((126.0 - jnp.log2(code.astype(F32))) * (1.0 / STEEP))


def marks(count, start):
    lane = lax.broadcasted_iota(jnp.int32, (count, 128), 1) - start
    row = lax.broadcasted_iota(jnp.int32, (count, 128), 0)
    return lane, (lane >= 0) & (lane < 24) & (lane % 8 == row % 8)


def bias_body(pair_ref, w_ref, out_ref, wide_ref, tops_ref):
    step = pl.program_id(0)

    @pl.when(step == 0)
    def _():
        wide_ref[...] = block_diagonal(w_ref, 8)

    lane, mark = marks(128, 0)
    for g in range(4):
        cols = jnp.concatenate([pair_ref[g * 8 + r] for r in range(8)], axis=1)
        t = lax.dot_general(wide_ref[...], cols, (((1,), (1,)), ((), ())), preferred_element_type=F32)
        code, top = encode(t * LOG2E)
        high = top.astype(BF16).astype(F32)
        middle = (top - high).astype(BF16).astype(F32)
        terms = jnp.where(lane < 8, high, jnp.where(lane < 16, middle, top - high - middle))
        tops_ref[step * 4 + g] = jnp.sum(jnp.where(mark, terms, 0.0).reshape(16, 8, 128), axis=1)
        if g % 2 == 0:
            even = code
            continue
        rows = pl.ds(pl.multiple_of(step * 32 + g * 8 - 8, 16), 16)
        for h in range(16):
            block = jnp.concatenate([even[h * 8:h * 8 + 8, :], code[h * 8:h * 8 + 8, :]], axis=0)
            out_ref[h, rows, :] = block
            out_ref[h + 16, rows, :] = block

    @pl.when(step == 1)
    def _():
        for h in range(16):
            tops = [tops_ref[g, h:h + 1, :] for g in range(8)]
            block = jnp.concatenate(tops + [jnp.zeros((8, 128), F32)], axis=0).astype(BF16)
            out_ref[h, 64:80, :] = block
            out_ref[h + 16, 64:80, :] = block


def bias_part(pair, w_pair):
    return pl.pallas_call(
        bias_body, grid=(2,), out_shape=pltpu.HBM((32, 80, 128), BF16),
        in_specs=[pl.BlockSpec((32, 128, 128), lambda i: (i, 0, 0)), pl.BlockSpec((16, 128), lambda i: (0, 0))],
        out_specs=pl.BlockSpec((32, 80, 128), lambda i: (0, 0, 0)),
        scratch_shapes=[pltpu.VMEM((128, 1024), BF16), pltpu.VMEM((8, 16, 128), F32)],
        compiler_params=pltpu.CompilerParams(vmem_limit_bytes=32 * 2**20), name="bias_part",
    )(pltpu.with_memory_space_constraint(pair, pltpu.HBM), pltpu.with_memory_space_constraint(w_pair, pltpu.HBM))


def unpack_body(x_ref, *out_refs):
    for e in range(2):
        for t in range(16):
            out_refs[e][t * 64:t * 64 + 64, :] = x_ref[e, t, :64]
        groups = []
        for group in range(4):
            tops = [x_ref[e, group * 4 + n, 64:80].astype(F32)[:8, :32] for n in range(4)]
            groups.append(jnp.concatenate(tops, axis=1))
        out_refs[e][TOK:TOK + 32, :] = jnp.concatenate(groups, axis=0).astype(BF16)


def unpack(x):
    vm = pl.BlockSpec(memory_space=pltpu.VMEM)
    return pl.pallas_call(
        unpack_body, out_shape=[jax.ShapeDtypeStruct((TOK + 32, 128), BF16)] * 2, in_specs=[vm], out_specs=[vm] * 2,
        compiler_params=pltpu.CompilerParams(vmem_limit_bytes=16 * 2**20), name="unpack",
    )(x)


def gpair_body(x_ref, w_ref, out_ref, wide_ref):
    step = pl.program_id(0)

    @pl.when(step == 0)
    def _():
        wide_ref[...] = block_diagonal(w_ref, 16)

    for g in range(2):
        rows = pl.ds(pl.multiple_of(step * 32 + g * 16, 16), 16)
        x = (x_ref[0, :, rows, :].astype(F32) + x_ref[1, :, rows, :].astype(F32)).astype(BF16).reshape(256, 128)
        t = lax.dot_general(x, wide_ref[...], (((0,), (0,)), ((), ())), preferred_element_type=F32)
        for r in range(16):
            out_ref[g * 16 + r] = t[:, r * 128:r * 128 + 128].astype(BF16)


def gpair(x, w_pair):
    vm = pl.BlockSpec(memory_space=pltpu.VMEM)
    return pl.pallas_call(
        gpair_body, grid=(2,), out_shape=jax.ShapeDtypeStruct((64, 128, 128), BF16),
        in_specs=[vm, vm], out_specs=pl.BlockSpec((32, 128, 128), lambda i: (i, 0, 0)),
        scratch_shapes=[pltpu.VMEM((256, 2048), BF16)],
        compiler_params=pltpu.CompilerParams(vmem_limit_bytes=32 * 2**20), name="gpair",
    )(x, w_pair)


def project_body(x_ref, c_ref, wq_ref, wk_ref, wv_ref, wo_ref, out_ref):
    x = x_ref[...].reshape(NB * 64, WIDTH)
    c = c_ref[...].reshape(NB * 64, WIDTH)
    for slot, w_ref in enumerate((wq_ref, wk_ref, wv_ref)):
        t = jnp.dot(x, w_ref[...], preferred_element_type=F32).T.astype(BF16)
        for h in range(HEADS):
            out_ref[h, slot] = t[h * HD:h * HD + HD, :]
    t = lax.dot_general(wo_ref[...], c, (((1,), (1,)), ((), ())), preferred_element_type=F32).astype(BF16)
    for h in range(HEADS):
        out_ref[h, 3] = t[h * HD:h * HD + HD, :]


def project(single, cotangent, w_query, w_key, w_value, w_out):
    vm = pl.BlockSpec(memory_space=pltpu.VMEM)
    return pl.pallas_call(
        project_body, out_shape=jax.ShapeDtypeStruct((HEADS, 4, HD, NB * 64), BF16),
        in_specs=[vm] * 6, out_specs=vm,
        compiler_params=pltpu.CompilerParams(vmem_limit_bytes=40 * 2**20), name="project",
    )(single, cotangent, w_query, w_key, w_value, w_out)


def final_body(g_ref, wq_ref, wk_ref, wv_ref, out_ref):
    total = None
    for slot, w_ref in enumerate((wq_ref, wk_ref, wv_ref)):
        part = jnp.dot(w_ref[...], g_ref[:, slot].reshape(WIDTH, NB * 64), preferred_element_type=F32)
        total = part if total is None else total + part
    out_ref[...] = total.T.astype(BF16).reshape(NB, 64, WIDTH)


def final(g, w_query, w_key, w_value):
    vm = pl.BlockSpec(memory_space=pltpu.VMEM)
    return pl.pallas_call(
        final_body, out_shape=jax.ShapeDtypeStruct((NB, 64, WIDTH), BF16),
        in_specs=[vm] * 4, out_specs=vm,
        compiler_params=pltpu.CompilerParams(vmem_limit_bytes=40 * 2**20), name="final",
    )(g, w_query, w_key, w_value)


def shift_y(x, d):
    return lax.ppermute(x, "sample", [(i, ((i // 2 + d) % 4) * 2 + i % 2) for i in range(8)])


def exchange(x):
    groups = [[(2 * y + e) * 16 + t for e in range(2) for t in range(16)] for y in range(4)]
    return lax.all_to_all(x, ("sample", "tok"), 0, 0, axis_index_groups=groups)


def gather_blocks(own):
    up0, down1 = shift_y(own[0], 1), shift_y(own[1], -1)
    up1, down0 = shift_y(own[1], 1), shift_y(own[0], -1)
    return [own[0], own[1], up0, up1, down0, down1, shift_y(up0, 1), shift_y(down1, -1)]


def key_order():
    y = lax.axis_index("sample") // 2
    return jnp.stack([((y + d) % 4) * 2 + e for d in (0, 3, 1, 2) for e in (0, 1)]).astype(jnp.int32)


def plus(*terms):
    total = terms[0].astype(F32)
    for term in terms[1:]:
        total = total + term.astype(F32)
    return total.astype(BF16)


def scatter_blocks(blocks):
    own0, own1, down0, down1, up0, up1, far0, far1 = blocks
    far0, far1 = shift_y(far0, 1), shift_y(far1, -1)
    up1, down0 = shift_y(up1, 1), shift_y(down0, -1)
    up0, down1 = shift_y(plus(up0, far0), 1), shift_y(plus(down1, far1), -1)
    return own_sum(own0, up0, down0, own1, up1, down1)


def own_sum_body(a0, b0, c0, a1, b1, c1, out_ref):
    out_ref[0] = plus(a0[...], b0[...], c0[...])
    out_ref[1] = plus(a1[...], b1[...], c1[...])


def own_sum(*terms):
    vm = pl.BlockSpec(memory_space=pltpu.VMEM)
    return pl.pallas_call(
        own_sum_body, out_shape=jax.ShapeDtypeStruct((2, TOK, 128), BF16), in_specs=[vm] * 6, out_specs=vm,
        compiler_params=pltpu.CompilerParams(vmem_limit_bytes=16 * 2**20), name="own_sum",
    )(*terms)


def local(single, pair, w_query, w_key, w_value, w_out, w_pair, cotangent):
    order = key_order()
    sent = project(single, cotangent, w_query, w_key, w_value, w_out)
    bias = exchange(bias_part(pair, w_pair.T))
    bias, sent = lax.optimization_barrier((bias, sent))
    received = lax.all_to_all(sent, "tok", 0, 0)
    blocks = gather_blocks(unpack(bias.reshape(2, 16, 80, 128)))
    received, ready = lax.optimization_barrier((received, early([blocks[u] for u in EARLY[:4]]) + early([blocks[u] for u in EARLY[4:]])))
    dbias, grads = attend(order, ready, [blocks[u] for u in LATE], prep(order, received))
    grads = lax.all_to_all(grads, "tok", 0, 0)
    dbias = scatter_blocks(dbias)
    grads, dbias = lax.optimization_barrier((grads, dbias))
    grad_single = final(grads, w_query, w_key, w_value)
    dbias = exchange(dbias.reshape(32, 64, 128)).reshape(2, 16, 64, 128)
    return (grad_single, gpair(dbias, w_pair.T))


def solution(mesh):
    rows, keys = P("sample", "tok", None), P("tok", "sample", None)
    return jax.shard_map(
        local, mesh=mesh, in_specs=(rows, keys, P(), P(), P(), P(), P(), rows),
        out_specs=(rows, keys), check_vma=False,
    )
```
